32 devices in a mesh: dom: 4 (over z), cls: 8 (over y, x, core).
Axes of the slice: x: 2, y: 2, z: 4, core: 2. Of those that a mesh axis runs over, the one named last changes fastest.
Arguments:
- images: bfloat16 [1024, 64, 256], P(('dom', 'cls'))
- references: bfloat16 [128, 64, 256], P('cls')
- ctf_table: float32 [64, 64], replicated, may hold values from 0.2 to 1
- defocus: int32 [1024], P(('dom', 'cls')), may hold values from 0 to 63
- priors: int32 [1024, 8], P(('dom', 'cls')), may hold values from 0 to 127, as said below
Outputs:
- new_refs: float32 [128, 64, 256], P('cls', 'dom')
The draws below stay inside these ranges and needn't reach their ends.
Inputs may be any that keep to these rules, and one draw needn't show every extreme that they name: `priors`: the owner of class k is index k // 16 of cls. Among the prior entries of one device's particles at most 40 name classes of any one owner; in each index of dom one owner is named exactly 40 times by every device.
All inputs are finite; a program needn't handle non-finite values.
Results may differ from the reference program's by a relative error of at most 0.011.
Values may be sent and summed in bfloat16 or wider, within the bound.
A program may use at most 128 MiB of HBM per device.

```python
import math
import jax
import jax.numpy as jnp
from jax import lax

CYCLES = 64
ANGLES = 256
HARM = 128
PRIOR = 8
CLS_DEV = 16
CLASSES = 128
GROUPS = 64
NP_DEV = 32
PARTICLES = 1024
CAP = 40
N_DOM = 4
N_CLS = 8


def prior_table(key):
    blocks = N_DOM * N_CLS
    per_block = NP_DEV * PRIOR
    seats = N_CLS * CAP
    hot_owner = jax.random.randint(jax.random.fold_in(key, 101), (N_DOM,), 0, N_CLS)
    hot_block = jnp.repeat(hot_owner, N_CLS)
    block_keys = jax.random.split(jax.random.fold_in(key, 102), blocks)

    def one_block(block_key, hottest):
        key_seat, key_order, key_class = jax.random.split(block_key, 3)
        others = jax.random.permutation(key_seat, seats - CAP).astype(jnp.int32)
        chosen = jnp.concatenate([jnp.arange(CAP, dtype=jnp.int32), CAP + others[:per_block - CAP]])
        owner = (chosen // CAP + hottest) % N_CLS
        owner = jax.random.permutation(key_order, owner)
        within = jax.random.randint(key_class, (per_block,), 0, CLS_DEV)
        return owner * CLS_DEV + within
    return jax.vmap(one_block)(block_keys, hot_block).reshape(PARTICLES, PRIOR).astype(jnp.int32)


def reference_table(key):
    spread = 4.7 / math.sqrt(CYCLES * ANGLES)
    return spread * jax.random.normal(jax.random.fold_in(key, 201), (CLASSES, CYCLES, ANGLES), jnp.float32)


def draw_priors(key, part):
    return prior_table(key)


def draw_references(key, part):
    table = reference_table(key)
    return table.astype(jnp.bfloat16)


def draw_images(key, part):
    image = jax.random.normal(jax.random.fold_in(key, 302), (PARTICLES, CYCLES, ANGLES), jnp.float32)
    return image.astype(jnp.bfloat16)


def set_ends(entries, rng, smallest, high):
    extent = entries.shape
    index_at = [jax.random.randint(jax.random.fold_in(rng, axis), (), 0, extent[axis]) for axis in range(len(extent))]
    entries = entries.at[tuple(index_at)].set(smallest)
    longest = extent.index(max(extent))
    index_at[longest] = (index_at[longest] + 1) % extent[longest]
    return entries.at[tuple(index_at)].set(high)


def setup_inputs(seed: int = 0) -> dict:
    splits = jax.random.split(jax.random.key(seed), 6)
    images = draw_images(jax.random.fold_in(splits[5], 71), 0)
    references = draw_references(jax.random.fold_in(splits[5], 71), 0)
    ctf_table = jnp.clip(jax.random.uniform(splits[2], (GROUPS, CYCLES), jnp.float32, 0.2, 1.0), 0.2, 1.0)
    defocus = set_ends(jax.random.randint(splits[3], (PARTICLES,), 0, GROUPS), jax.random.fold_in(splits[3], 1), 0, GROUPS - 1).astype(jnp.int32)
    priors = draw_priors(jax.random.fold_in(splits[5], 71), 0)
    return dict(images=images, references=references, ctf_table=ctf_table, defocus=defocus, priors=priors)


def angle_tables(angles):
    harm_count = angles // 2
    angle_index = jnp.arange(angles, dtype=jnp.int32)
    harm_index = jnp.arange(harm_count, dtype=jnp.int32)
    phase_grid = (angle_index[:, None] * harm_index[None, :]) % angles
    angle_grid = (2.0 * jnp.pi / angles) * phase_grid.astype(jnp.float32)
    cosine = jnp.cos(angle_grid)
    sine_grid = jnp.sin(angle_grid)
    forward = jnp.concatenate([cosine, sine_grid], axis=1)
    harm_weight = jnp.where(harm_index == 0, 1.0, 2.0).astype(jnp.float32) / angles
    inverse = jnp.concatenate([cosine.T * harm_weight[:, None], -sine_grid.T * harm_weight[:, None]], axis=0)
    return forward, inverse


def to_harmonics(frames, forward):
    frame_count, cycle_count, angles = frames.shape
    flat_rows = jnp.dot(frames.reshape(frame_count * cycle_count, angles), forward.astype(jnp.bfloat16), preferred_element_type=jnp.float32)
    return flat_rows.astype(jnp.bfloat16).reshape(frame_count, cycle_count, forward.shape[1])


def slot_scores(part_block, ref_block, ctf_block, inverse):
    harm_count = part_block.shape[2] // 2
    part_cos = part_block[:, :, :harm_count].astype(jnp.float32)
    part_sin = part_block[:, :, harm_count:].astype(jnp.float32)
    ref_cos = ref_block[:, :, :harm_count].astype(jnp.float32)
    ref_sin = ref_block[:, :, harm_count:].astype(jnp.float32)
    ctf_weight = ctf_block[:, :, None]
    real_part = jnp.sum(ctf_weight * (part_cos * ref_cos + part_sin * ref_sin), axis=1)
    imag_part = jnp.sum(ctf_weight * (part_cos * ref_sin - part_sin * ref_cos), axis=1)
    joined = jnp.concatenate([real_part, imag_part], axis=1)
    return jnp.dot(joined, inverse, precision=lax.Precision.HIGHEST)


def accumulate_terms(part_block, weights, ctf_block, forward):
    harm_count = part_block.shape[2] // 2
    spectrum = jnp.dot(weights, forward, precision=lax.Precision.HIGHEST)
    w_cos = spectrum[:, None, :harm_count]
    w_sin = spectrum[:, None, harm_count:]
    part_cos = part_block[:, :, :harm_count].astype(jnp.float32)
    part_sin = part_block[:, :, harm_count:].astype(jnp.float32)
    ctf_weight = ctf_block[:, :, None]
    real_part = ctf_weight * (part_cos * w_cos + part_sin * w_sin)
    imag_part = ctf_weight * (part_sin * w_cos - part_cos * w_sin)
    term_rows = jnp.concatenate([real_part, imag_part], axis=2)
    norm_rows = ctf_block * ctf_block * jnp.sum(weights, axis=1)[:, None]
    return term_rows, norm_rows


def reference(images, references, ctf_table, defocus, priors):
    forward, inverse = angle_tables(ANGLES)
    ref_harm = to_harmonics(references, forward)
    block_size = 64
    block_count = PARTICLES // block_size
    image_blocks = images.reshape(block_count, block_size, CYCLES, ANGLES)
    group_blocks = defocus.reshape(block_count, block_size)
    prior_blocks = priors.reshape(block_count, block_size, PRIOR)

    def scan_step(carry, inputs):
        class_sums, class_norms = carry
        frames, groups, classes = inputs
        harmonic = to_harmonics(frames, forward)
        part_block = jnp.repeat(harmonic, PRIOR, axis=0)
        flat_class = classes.reshape(-1).astype(jnp.int32)
        ref_block = ref_harm[flat_class]
        ctf_block = jnp.repeat(ctf_table[groups], PRIOR, axis=0)
        scores = slot_scores(part_block, ref_block, ctf_block, inverse)
        grouped = scores.reshape(block_size, PRIOR * ANGLES)
        highest = jnp.max(grouped, axis=1, keepdims=True)
        log_total = highest + jnp.log(jnp.sum(jnp.exp(grouped - highest), axis=1, keepdims=True))
        weights = jnp.exp(grouped - log_total).reshape(block_size * PRIOR, ANGLES)
        term_rows, norm_rows = accumulate_terms(part_block, weights, ctf_block, forward)
        return (class_sums.at[flat_class].add(term_rows), class_norms.at[flat_class].add(norm_rows)), None

    initial = (jnp.zeros((CLASSES, CYCLES, 2 * HARM), jnp.float32), jnp.zeros((CLASSES, CYCLES), jnp.float32))
    (class_sums, class_norms), ignored = lax.scan(scan_step, initial, (image_blocks, group_blocks, prior_blocks))
    return class_sums / (class_norms + 1.0)[:, :, None]
```

```python
import functools

import jax
import jax.numpy as jnp
import numpy as np
from jax import lax
from jax.experimental import pallas as pl
from jax.experimental.pallas import tpu as pltpu
from jax.sharding import PartitionSpec as P

MESH = pl.DeviceIdType.MESH
VMEM = pl.BlockSpec(memory_space=pltpu.VMEM)
ANY = pl.BlockSpec(memory_space=pl.ANY)
LIMIT = 56 * 1024 * 1024
F32 = jnp.float32
BF16 = jnp.bfloat16
EXACT = lax.Precision.HIGHEST


def angle_tables(angles):
    harm_count = angles // 2
    phase = np.arange(angles)[:, None] * np.arange(harm_count)[None, :] % angles
    grid = 2.0 * np.pi / angles * phase
    cosine, sine = np.cos(grid), np.sin(grid)
    forward = np.concatenate([cosine, sine], axis=1)
    weight = np.where(np.arange(harm_count) == 0, 1.0, 2.0)[:, None] / angles
    inverse = np.concatenate([cosine.T * weight, -sine.T * weight], axis=0)
    return forward.astype(np.float32), inverse.astype(np.float32)


def compute_call(body, out_shape, inputs, scratch=()):
    return pl.pallas_call(
        body,
        out_shape=out_shape,
        in_specs=[VMEM] * len(inputs),
        out_specs=jax.tree.map(lambda _: VMEM, out_shape),
        scratch_shapes=list(scratch),
        compiler_params=pltpu.CompilerParams(vmem_limit_bytes=LIMIT),
    )(*inputs)


def harmonics_body(owners, cycles, img_ref, ref_ref, table_ref, part_ref, cls_ref, low, high):
    harm = table_ref.shape[1] // 2
    share = cycles // owners
    for src, dst in ((img_ref, part_ref), (ref_ref, cls_ref)):
        rows = src.shape[0]
        frames = rows // cycles
        step = min(256, rows)

        @pl.loop(0, rows // step)
        def _(b):
            at = pl.ds(pl.multiple_of(b * step, step), step)
            out = jnp.dot(src[at, :], table_ref[...], preferred_element_type=F32)
            low[at, :] = out[:, :harm]
            high[at, :] = out[:, harm:]

        for cycle in range(cycles):
            at = pl.ds(cycle, frames, stride=cycles)
            place = cycle % owners * share + cycle // owners
            dst[place, :, :harm] = low[at, :].astype(BF16)
            dst[place, :, harm:] = high[at, :].astype(BF16)


def greet(peers):
    barrier = pltpu.get_barrier_semaphore()
    for peer in peers:
        pl.semaphore_signal(barrier, inc=1, device_id=peer, device_id_type=MESH)
    pl.semaphore_wait(barrier, len(peers))


def exchange_body(owners, spread, *refs):
    count = len(spread)
    ins, outs = refs[:count], refs[count : 2 * count]
    send_sem, recv_sem, local_sem = refs[2 * count :]
    dom, me = lax.axis_index("dom"), lax.axis_index("cls")
    peers = [(dom, lax.rem(me + off, owners)) for off in range(1, owners)]
    greet(peers)
    copies = []
    for off, peer in enumerate(peers, 1):
        for a in range(count):
            copy = pltpu.make_async_remote_copy(
                src_ref=ins[a] if spread[a] else ins[a].at[peer[1]],
                dst_ref=outs[a].at[me],
                send_sem=send_sem.at[off, a],
                recv_sem=recv_sem.at[off, a],
                device_id=peer,
                device_id_type=MESH,
            )
            copy.start()
            copies.append(copy)
    for a in range(count):
        copy = pltpu.make_async_copy(
            ins[a] if spread[a] else ins[a].at[me], outs[a].at[me], local_sem.at[a]
        )
        copy.start()
        copies.append(copy)
    for copy in copies:
        copy.wait()


def exchange(owners, number, arrays, spread):
    count = len(arrays)
    shapes = [
        jax.ShapeDtypeStruct((owners,) + (a.shape if s else a.shape[1:]), a.dtype)
        for a, s in zip(arrays, spread)
    ]
    return pl.pallas_call(
        functools.partial(exchange_body, owners, spread),
        out_shape=shapes,
        in_specs=[ANY] * count,
        out_specs=[ANY] * count,
        scratch_shapes=[
            pltpu.SemaphoreType.DMA((owners, count)),
            pltpu.SemaphoreType.DMA((owners, count)),
            pltpu.SemaphoreType.DMA((count,)),
        ],
        compiler_params=pltpu.CompilerParams(collective_id=number, has_side_effects=True),
    )(*arrays)


def ctf_rows(meta, priors, table_ref):
    groups = table_ref.shape[0]
    group = meta[:, priors : priors + 1]
    hits = (group == lax.broadcasted_iota(jnp.int32, (meta.shape[0], groups), 1)).astype(F32)
    return jnp.dot(hits, table_ref[...], precision=EXACT, preferred_element_type=F32)


def column(rows, index):
    lanes = lax.broadcasted_iota(jnp.int32, rows.shape, 1)
    return jnp.sum(jnp.where(lanes == index, rows, 0.0), axis=1, keepdims=True)


def weighted_parts(part_ref, ctf, owners, scaled):
    me = lax.axis_index("cls")
    share = part_ref.shape[1]
    for i in range(share):
        frames = part_ref[:, i].reshape(-1, part_ref.shape[3]).astype(F32)
        scaled[i] = frames * column(ctf, me + owners * i)


def class_hits(meta, j, classes):
    picked = column(meta.astype(F32), j)
    lanes = lax.broadcasted_iota(jnp.int32, (meta.shape[0], classes), 1)
    return (picked.astype(jnp.int32) == lanes).astype(F32)


def score_body(owners, priors, part_ref, cls_ref, meta_ref, table_ref, out_ref, scaled):
    share, width = part_ref.shape[1], part_ref.shape[3]
    harm = width // 2
    classes = owners * cls_ref.shape[2]
    frames = part_ref.shape[2]
    meta = meta_ref[...].reshape(-1, meta_ref.shape[2])
    weighted_parts(part_ref, ctf_rows(meta, priors, table_ref), owners, scaled)

    @pl.loop(0, priors)
    def _(j):
        hits = class_hits(meta_ref[...].reshape(-1, meta_ref.shape[2]), j, classes).astype(BF16)
        real, imag = 0.0, 0.0
        for i in range(share):
            picked = jnp.dot(
                hits, cls_ref[:, i].reshape(classes, width), preferred_element_type=F32
            )
            pc, ps = scaled[i, :, :harm], scaled[i, :, harm:]
            cc, cs = picked[:, :harm], picked[:, harm:]
            real = real + (pc * cc + ps * cs)
            imag = imag + (pc * cs - ps * cc)
        out_ref[:, j, :, :harm] = real.astype(BF16).reshape(owners, frames, harm)
        out_ref[:, j, :, harm:] = imag.astype(BF16).reshape(owners, frames, harm)


def weight_body(owners, got_ref, forward_ref, inverse_ref, out_ref):
    priors, frames, width = got_ref.shape[1:]
    joined = got_ref[0].astype(F32)
    for src in range(1, owners):
        joined = joined + got_ref[src].astype(F32)
    joined = joined.reshape(priors * frames, width)
    scores = jnp.dot(joined, inverse_ref[...], precision=EXACT, preferred_element_type=F32)
    scores = scores.reshape(priors, frames, -1)
    highest = jnp.max(jnp.max(scores, axis=0), axis=1, keepdims=True)
    total = jnp.sum(jnp.sum(jnp.exp(scores - highest[None]), axis=0), axis=1, keepdims=True)
    log_total = highest + jnp.log(total)
    weights = jnp.exp(scores - log_total[None]).reshape(priors * frames, -1)
    spectrum = jnp.dot(weights, forward_ref[...], precision=EXACT, preferred_element_type=F32)
    out_ref[...] = spectrum.astype(BF16).reshape(out_ref.shape)


def sum_body(
    owners, priors, spec_ref, part_ref, meta_ref, table_ref, out_ref, norm_ref, scaled, sums, norms
):
    share, width = part_ref.shape[1], part_ref.shape[3]
    harm = width // 2
    owned = norm_ref.shape[0]
    classes = owners * owned
    meta = meta_ref[...].reshape(-1, meta_ref.shape[2])
    ctf = ctf_rows(meta, priors, table_ref)
    weighted_parts(part_ref, ctf, owners, scaled)
    ctf_square = ctf * ctf
    sums[...] = jnp.zeros_like(sums)
    norms[...] = jnp.zeros_like(norms)

    @pl.loop(0, priors)
    def _(j):
        hits = class_hits(meta_ref[...].reshape(-1, meta_ref.shape[2]), j, classes).T
        spectrum = spec_ref[:, j].reshape(-1, width).astype(F32)
        wc, ws = spectrum[:, :harm], spectrum[:, harm:]
        norms[...] += jnp.dot(
            hits, ctf_square * wc[:, :1], precision=EXACT, preferred_element_type=F32
        )
        hits = hits.astype(BF16)
        for i in range(share):
            pc, ps = scaled[i, :, :harm], scaled[i, :, harm:]
            terms = jnp.concatenate([pc * wc + ps * ws, ps * wc - pc * ws], axis=1)
            sums[i] += jnp.dot(hits, terms.astype(BF16), preferred_element_type=F32)

    out_ref[...] = sums[...].astype(BF16)
    mine = pl.multiple_of(lax.axis_index("cls") * owned, owned)
    norm_ref[...] = norms[pl.ds(mine, owned), :]


def deliver_body(doms, owners, sum_ref, norm_ref, got_ref, norm_got, sems, norm_sems, local):
    run, owned = got_ref.shape[1:3]
    dom, me = lax.axis_index("dom"), lax.axis_index("cls")
    offsets = [(a, b) for a in range(doms) for b in range(owners) if (a, b) != (0, 0)]
    peers = [(lax.rem(dom + a, doms), lax.rem(me + b, owners)) for a, b in offsets]
    greet(peers)

    def block(index):
        start = pl.multiple_of(index[1] * owned, owned)
        return sum_ref.at[pl.ds(index[0] * run, run), pl.ds(start, owned), :]

    copies = []
    for (a, b), peer in zip(offsets, peers):
        copies.append(
            pltpu.make_async_remote_copy(
                src_ref=block(peer),
                dst_ref=got_ref.at[dom * owners + me],
                send_sem=sems.at[0, a, b],
                recv_sem=sems.at[1, a, b],
                device_id=peer,
                device_id_type=MESH,
            )
        )
        if b == 0:
            copies.append(
                pltpu.make_async_remote_copy(
                    src_ref=norm_ref,
                    dst_ref=norm_got.at[dom],
                    send_sem=norm_sems.at[0, a],
                    recv_sem=norm_sems.at[1, a],
                    device_id=peer,
                    device_id_type=MESH,
                )
            )
    copies.append(
        pltpu.make_async_copy(block((dom, me)), got_ref.at[dom * owners + me], local.at[0])
    )
    copies.append(pltpu.make_async_copy(norm_ref, norm_got.at[dom], local.at[1]))
    for copy in copies:
        copy.start()
    for copy in copies:
        copy.wait()


def deliver(doms, owners, sums, norms):
    share, classes, width = sums.shape
    owned = norms.shape[0]
    run = share // doms
    return pl.pallas_call(
        functools.partial(deliver_body, doms, owners),
        out_shape=[
            jax.ShapeDtypeStruct((doms * owners, run, owned, width), BF16),
            jax.ShapeDtypeStruct((doms,) + norms.shape, F32),
        ],
        in_specs=[ANY] * 2,
        out_specs=[ANY] * 2,
        scratch_shapes=[
            pltpu.SemaphoreType.DMA((2, doms, owners)),
            pltpu.SemaphoreType.DMA((2, doms)),
            pltpu.SemaphoreType.DMA((2,)),
        ],
        compiler_params=pltpu.CompilerParams(collective_id=4, has_side_effects=True),
    )(sums, norms)


def finish_body(doms, owners, got_ref, norm_ref, out_ref, low, high):
    run, owned, width = got_ref.shape[1:]
    harm = width // 2
    held = run * owners
    norms = norm_ref[0]
    for a in range(1, doms):
        norms = norms + norm_ref[a]
    first = lax.axis_index("dom") * held
    for i in range(run):
        for c in range(owners):
            total = got_ref[c, i].astype(F32)
            for a in range(1, doms):
                total = total + got_ref[a * owners + c, i].astype(F32)
            cycle = c + owners * i
            result = total / (column(norms, first + cycle) + 1.0)
            at = pl.ds(cycle, owned, stride=held)
            low[at, :] = result[:, :harm]
            high[at, :] = result[:, harm:]
    out_ref[:, :harm] = low[...]
    out_ref[:, harm:] = high[...]


def on_device(doms, images, references, ctf_table, defocus, priors):
    owners = lax.axis_size("cls")
    particles, cycles, angles = images.shape
    owned = references.shape[0]
    classes = owners * owned
    prior_count = priors.shape[1]
    share = cycles // owners
    width = angles // 2 * 2
    group = owners * particles
    forward, inverse = (jnp.asarray(t) for t in angle_tables(angles))
    meta = jnp.concatenate(
        [priors, defocus[:, None], jnp.zeros((particles, 127 - prior_count), jnp.int32)], axis=1
    )

    part_send, cls_send = compute_call(
        functools.partial(harmonics_body, owners, cycles),
        [
            jax.ShapeDtypeStruct((cycles, particles, width), BF16),
            jax.ShapeDtypeStruct((cycles, owned, width), BF16),
        ],
        (
            images.reshape(particles * cycles, angles),
            references.reshape(owned * cycles, angles),
            forward.astype(BF16),
        ),
        [pltpu.VMEM((max(particles, owned) * cycles, width // 2), F32)] * 2,
    )
    part, cls, meta = exchange(
        owners,
        1,
        (
            part_send.reshape(owners, share, particles, width),
            cls_send.reshape(owners, share, owned, width),
            meta,
        ),
        (False, False, True),
    )
    partial = compute_call(
        functools.partial(score_body, owners, prior_count),
        jax.ShapeDtypeStruct((owners, prior_count, particles, width), BF16),
        (part, cls, meta, ctf_table),
        [pltpu.VMEM((share, group, width), F32)],
    )
    (got,) = exchange(owners, 2, (partial,), (False,))
    spectrum = compute_call(
        functools.partial(weight_body, owners),
        jax.ShapeDtypeStruct((prior_count, particles, width), BF16),
        (got, forward, inverse),
    )
    (spectra,) = exchange(owners, 3, (spectrum,), (True,))
    sums, norms = compute_call(
        functools.partial(sum_body, owners, prior_count),
        [
            jax.ShapeDtypeStruct((share, classes, width), BF16),
            jax.ShapeDtypeStruct((owned, cycles), F32),
        ],
        (spectra, part, meta, ctf_table),
        [
            pltpu.VMEM((share, group, width), F32),
            pltpu.VMEM((share, classes, width), F32),
            pltpu.VMEM((classes, cycles), F32),
        ],
    )
    held = cycles // doms
    if held % owners == 0:
        norms = jnp.pad(norms, ((0, 0), (0, 128 - cycles)))
        got, norms = deliver(doms, owners, sums, norms)
        out = compute_call(
            functools.partial(finish_body, doms, owners),
            jax.ShapeDtypeStruct((owned * held, width), F32),
            (got, norms),
            [pltpu.VMEM((owned * held, width // 2), F32)] * 2,
        )
        return out.reshape(owned, held, width)
    mine = lax.axis_index("cls") + owners * jnp.arange(share)
    placed = jnp.zeros((cycles, classes, width), F32).at[mine].set(sums.astype(F32))
    placed = lax.psum_scatter(placed, "dom", scatter_dimension=0, tiled=True)
    placed = lax.psum_scatter(placed, "cls", scatter_dimension=1, tiled=True)
    norms = lax.psum_scatter(norms, "dom", scatter_dimension=1, tiled=True)
    return placed.transpose(1, 0, 2) / (norms + 1.0)[:, :, None]


def solution(mesh):
    return jax.shard_map(
        functools.partial(on_device, mesh.shape["dom"]),
        mesh=mesh,
        in_specs=(
            P(("dom", "cls"), None, None),
            P("cls", None, None),
            P(),
            P(("dom", "cls")),
            P(("dom", "cls"), None),
        ),
        out_specs=P("cls", "dom", None),
        check_vma=False,
    )
```

```python
import functools

import jax
import jax.numpy as jnp
import numpy as np
from jax import lax
from jax.experimental import pallas as pl
from jax.experimental.pallas import tpu as pltpu
from jax.sharding import PartitionSpec as P

MESH = pl.DeviceIdType.MESH
VMEM = pl.BlockSpec(memory_space=pltpu.VMEM)
LIMIT = 56 * 1024 * 1024
F32 = jnp.float32
BF16 = jnp.bfloat16
EXACT = lax.Precision.HIGHEST
TILE = 16


def angle_tables(angles):
    harm_count = angles // 2
    phase = np.arange(angles)[:, None] * np.arange(harm_count)[None, :] % angles
    grid = 2.0 * np.pi / angles * phase
    cosine, sine = np.cos(grid), np.sin(grid)
    forward = np.concatenate([cosine, sine], axis=1)
    weight = np.where(np.arange(harm_count) == 0, 1.0, 2.0)[:, None] / angles
    inverse = np.concatenate([cosine.T * weight, -sine.T * weight], axis=0)
    return forward.astype(np.float32), inverse.astype(np.float32)


def swap_matrix():
    rows = np.arange(TILE * TILE)
    swap = np.zeros((TILE * TILE, TILE * TILE), np.float32)
    swap[rows, rows % TILE * TILE + rows // TILE] = 1.0
    return swap


def harmonics(src, dst, swap, table, owners):
    frames, cycles, angles = src.shape
    for first in range(0, cycles, TILE):
        for frame in range(0, frames, TILE):
            block = src[frame : frame + TILE, first : first + TILE, :]
            block = block.reshape(TILE * TILE, angles)
            block = jnp.dot(swap, block, preferred_element_type=F32).astype(BF16)
            out = jnp.dot(block, table, preferred_element_type=F32).astype(BF16)
            for r in range(TILE):
                cycle = first + r
                dst[cycle % owners, cycle // owners, frame : frame + TILE, :] = out[
                    r * TILE : (r + 1) * TILE
                ]


def column(rows, index):
    lanes = lax.broadcasted_iota(jnp.int32, rows.shape, 1)
    return jnp.sum(jnp.where(lanes == index, rows, 0.0), axis=1, keepdims=True)


def class_hits(meta, priors, classes):
    lanes = lax.broadcasted_iota(jnp.int32, (meta.shape[0], classes), 1)
    return jnp.concatenate(
        [(meta[:, j : j + 1] == lanes).astype(F32) for j in range(priors)], axis=0
    )


def ctf_rows(meta, priors, table):
    groups = table.shape[0]
    lanes = lax.broadcasted_iota(jnp.int32, (meta.shape[0], groups), 1)
    hits = (meta[:, priors : priors + 1] == lanes).astype(F32)
    return jnp.dot(hits, table, precision=EXACT, preferred_element_type=F32)


def body(
    doms,
    owners,
    priors,
    deliver,
    img_ref,
    ref_ref,
    meta_ref,
    ctf_ref,
    swap_ref,
    forward_ref,
    inverse_ref,
    *rest,
):
    if deliver:
        out_ref, rest = rest[0], rest[1:]
    else:
        sum_out, norm_out, rest = rest[0], rest[1], rest[2:]
    (
        part_send,
        part_got,
        cls_send,
        cls_got,
        meta_got,
        scaled,
        ctf_got,
        score_send,
        score_got,
        spec_send,
        spec_got,
        sums,
        norms,
        sum_send,
        sum_got,
        norm_send,
        norm_got,
        low,
        high,
        cls_sem,
        meta_sem,
        part_sem,
        score_sem,
        spec_sem,
        sum_sem,
        norm_sem,
    ) = rest
    dom, me = lax.axis_index("dom"), lax.axis_index("cls")
    particles, cycles, angles = img_ref.shape
    owned = ref_ref.shape[0]
    classes = owners * owned
    share = cycles // owners
    harm = angles // 2
    width = 2 * harm

    barrier = pltpu.get_barrier_semaphore()
    offsets = [(a, b) for a in range(doms if deliver else 1) for b in range(owners)][1:]

    def peer(a, b):
        return (lax.rem(dom + a, doms), lax.rem(me + b, owners))

    def remote(src, dst, sem, place, device):
        return pltpu.make_async_remote_copy(
            src_ref=src,
            dst_ref=dst,
            send_sem=sem.at[(0,) + place],
            recv_sem=sem.at[(1,) + place],
            device_id=device,
            device_id_type=MESH,
        )

    def cls_copy(off):
        to = peer(0, off)
        return remote(cls_send.at[to[1]], cls_got.at[me], cls_sem, (off,), to)

    def meta_copy(off):
        return remote(meta_ref, meta_got.at[me], meta_sem, (off,), peer(0, off))

    def part_copy(off):
        to = peer(0, off)
        return remote(part_send.at[to[1]], part_got.at[me], part_sem, (off,), to)

    def score_copy(off):
        to = peer(0, owners - off)
        return remote(score_send.at[to[1]], score_got.at[me], score_sem, (off,), to)

    def spec_copy(off):
        return remote(spec_send, spec_got.at[me], spec_sem, (off,), peer(0, off))

    for a, b in offsets:
        pl.semaphore_signal(barrier, inc=1, device_id=peer(a, b), device_id_type=MESH)
    table = forward_ref[...].astype(BF16)
    swap = swap_ref[...]
    harmonics(ref_ref, cls_send, swap, table, owners)
    pl.semaphore_wait(barrier, len(offsets))
    for off in range(1, owners):
        meta_copy(off).start()
        cls_copy(off).start()
    harmonics(img_ref, part_send, swap, table, owners)
    for off in range(1, owners):
        part_copy(off).start()
    cls_got[me] = cls_send[me]
    part_got[me] = part_send[me]
    meta_got[me] = meta_ref[...]

    def score(src):
        meta = meta_got[src]
        ctf = ctf_rows(meta, priors, ctf_ref[...])
        ctf_got[src] = ctf
        hits = class_hits(meta, priors, classes).astype(BF16)
        real, imag = 0.0, 0.0
        for i in range(share):
            part = part_got[src, i].astype(F32) * column(ctf, me + owners * i)
            scaled[src, i] = part
            table = cls_got[:, i].reshape(classes, width)
            picked = jnp.dot(hits, table, preferred_element_type=F32)
            picked = picked.reshape(priors, particles, width)
            pc, ps = part[None, :, :harm], part[None, :, harm:]
            cc, cs = picked[:, :, :harm], picked[:, :, harm:]
            real = real + (pc * cc + ps * cs)
            imag = imag + (pc * cs - ps * cc)
        score_send[src, :, :, :harm] = real.astype(BF16)
        score_send[src, :, :, harm:] = imag.astype(BF16)

    for off in range(1, owners):
        meta_copy(off).wait()
        cls_copy(off).wait()

    @pl.loop(1, owners)
    def _(off):
        part_copy(off).wait_recv()
        score(lax.rem(me - off + owners, owners))
        score_copy(off).start()

    score(me)

    joined = score_send[me].astype(F32)
    for off in range(1, owners):
        score_copy(off).wait_recv()
        joined = joined + score_got[lax.rem(me + off, owners)].astype(F32)
    joined = joined.reshape(priors * particles, width)
    scores = jnp.dot(joined, inverse_ref[...], precision=EXACT, preferred_element_type=F32)
    scores = scores.reshape(priors, particles, angles)
    highest = jnp.max(jnp.max(scores, axis=0), axis=1, keepdims=True)
    total = jnp.sum(jnp.sum(jnp.exp(scores - highest[None]), axis=0), axis=1, keepdims=True)
    log_total = highest + jnp.log(total)
    weights = jnp.exp(scores - log_total[None]).reshape(priors * particles, angles)
    spectrum = jnp.dot(weights, forward_ref[...], precision=EXACT, preferred_element_type=F32)
    spec_send[...] = spectrum.astype(BF16).reshape(spec_send.shape)
    for off in range(1, owners):
        spec_copy(off).start()
    spec_got[me] = spec_send[...]
    sums[...] = jnp.zeros_like(sums)
    norms[...] = jnp.zeros_like(norms)

    def add(src):
        hits = class_hits(meta_got[src], priors, classes).T
        spectrum = spec_got[src].astype(F32)
        wc, ws = spectrum[:, :, :harm], spectrum[:, :, harm:]
        ctf = ctf_got[src]
        square = (ctf * ctf)[None] * wc[:, :, :1]
        norms[...] += jnp.dot(
            hits,
            square.reshape(priors * particles, cycles),
            precision=EXACT,
            preferred_element_type=F32,
        )
        hits = hits.astype(BF16)
        for i in range(share):
            part = scaled[src, i][None]
            pc, ps = part[:, :, :harm], part[:, :, harm:]
            terms = jnp.concatenate([pc * wc + ps * ws, ps * wc - pc * ws], axis=2)
            terms = terms.reshape(priors * particles, width).astype(BF16)
            sums[i] += jnp.dot(hits, terms, preferred_element_type=F32)

    add(me)

    @pl.loop(1, owners)
    def _(off):
        spec_copy(off).wait_recv()
        add(lax.rem(me - off + owners, owners))

    for off in range(1, owners):
        part_copy(off).wait_send()
        score_copy(off).wait_send()
        spec_copy(off).wait_send()

    mine = pl.multiple_of(me * owned, owned)
    if not deliver:
        sum_out[...] = sums[...].astype(BF16)
        norm_out[...] = norms[pl.ds(mine, owned), :]
        return

    run = share // doms
    held = cycles // doms
    sum_send[...] = sums[...].astype(BF16)
    norm_send[:, :cycles] = norms[pl.ds(mine, owned), :]

    def sum_copy(a, b):
        to = peer(a, b)
        start = pl.multiple_of(to[1] * owned, owned)
        src = sum_send.at[pl.ds(to[0] * run, run), pl.ds(start, owned), :]
        return remote(src, sum_got.at[dom, me], sum_sem, (a, b), to)

    def norm_copy(a):
        return remote(norm_send, norm_got.at[dom], norm_sem, (a,), peer(a, 0))

    order = sorted(offsets, key=lambda o: (o[0] == 0, abs(o[0] - doms // 2)))
    for a, b in order:
        sum_copy(a, b).start()
        if b == 0:
            norm_copy(a).start()
    sum_got[dom, me] = sum_send[pl.ds(dom * run, run), pl.ds(mine, owned), :]
    norm_got[dom] = norm_send[...]
    for a, b in offsets:
        sum_copy(a, b).wait()
        if b == 0:
            norm_copy(a).wait()
    total_norm = norm_got[0, :, :cycles]
    for a in range(1, doms):
        total_norm = total_norm + norm_got[a, :, :cycles]
    for i in range(run):
        for c in range(owners):
            cycle = c + owners * i
            result = sum_got[0, c, i].astype(F32)
            for a in range(1, doms):
                result = result + sum_got[a, c, i].astype(F32)
            result = result / (column(total_norm, dom * held + cycle) + 1.0)
            at = pl.ds(cycle, owned, stride=held)
            low[at, :] = result[:, :harm]
            high[at, :] = result[:, harm:]
    out_ref[:, :harm] = low[...]
    out_ref[:, harm:] = high[...]


def on_device(doms, images, references, ctf_table, defocus, priors):
    owners = lax.axis_size("cls")
    particles, cycles, angles = images.shape
    owned = references.shape[0]
    classes = owners * owned
    prior_count = priors.shape[1]
    share = cycles // owners
    width = angles // 2 * 2
    held = cycles // doms
    deliver = held % owners == 0
    run = max(share // doms, 1)
    forward, inverse = (jnp.asarray(t) for t in angle_tables(angles))
    swap = jnp.asarray(swap_matrix(), BF16)
    meta = jnp.concatenate(
        [priors, defocus[:, None], jnp.zeros((particles, 127 - prior_count), jnp.int32)], axis=1
    )
    if deliver:
        shapes = [jax.ShapeDtypeStruct((owned * held, width), F32)]
    else:
        shapes = [
            jax.ShapeDtypeStruct((share, classes, width), BF16),
            jax.ShapeDtypeStruct((owned, cycles), F32),
        ]
    slots = (prior_count, particles, width)
    sums = (share, classes, width)
    done = pl.pallas_call(
        functools.partial(body, doms, owners, prior_count, deliver),
        out_shape=shapes,
        in_specs=[VMEM] * 7,
        out_specs=[VMEM] * len(shapes),
        scratch_shapes=[
            pltpu.VMEM((owners, share, particles, width), BF16),
            pltpu.VMEM((owners, share, particles, width), BF16),
            pltpu.VMEM((owners, share, owned, width), BF16),
            pltpu.VMEM((owners, share, owned, width), BF16),
            pltpu.VMEM((owners,) + meta.shape, jnp.int32),
            pltpu.VMEM((owners, share, particles, width), F32),
            pltpu.VMEM((owners, particles, cycles), F32),
            pltpu.VMEM((owners,) + slots, BF16),
            pltpu.VMEM((owners,) + slots, BF16),
            pltpu.VMEM(slots, BF16),
            pltpu.VMEM((owners,) + slots, BF16),
            pltpu.VMEM(sums, F32),
            pltpu.VMEM((classes, cycles), F32),
            pltpu.VMEM(sums, BF16),
            pltpu.VMEM((doms, owners, run, owned, width), BF16),
            pltpu.VMEM((owned, 128), F32),
            pltpu.VMEM((doms, owned, 128), F32),
            pltpu.VMEM((owned * held, width // 2), F32),
            pltpu.VMEM((owned * held, width // 2), F32),
            pltpu.SemaphoreType.DMA((2, owners)),
            pltpu.SemaphoreType.DMA((2, owners)),
            pltpu.SemaphoreType.DMA((2, owners)),
            pltpu.SemaphoreType.DMA((2, owners)),
            pltpu.SemaphoreType.DMA((2, owners)),
            pltpu.SemaphoreType.DMA((2, doms, owners)),
            pltpu.SemaphoreType.DMA((2, doms)),
        ],
        compiler_params=pltpu.CompilerParams(
            collective_id=1, has_side_effects=True, vmem_limit_bytes=LIMIT
        ),
    )(images, references, meta, ctf_table, swap, forward, inverse)
    if deliver:
        return done[0].reshape(owned, held, width)
    sums, norms = done
    mine = lax.axis_index("cls") + owners * jnp.arange(share)
    placed = jnp.zeros((cycles, classes, width), F32).at[mine].set(sums.astype(F32))
    placed = lax.psum_scatter(placed, "dom", scatter_dimension=0, tiled=True)
    placed = lax.psum_scatter(placed, "cls", scatter_dimension=1, tiled=True)
    norms = lax.psum_scatter(norms, "dom", scatter_dimension=1, tiled=True)
    return placed.transpose(1, 0, 2) / (norms + 1.0)[:, :, None]


def solution(mesh):
    return jax.shard_map(
        functools.partial(on_device, mesh.shape["dom"]),
        mesh=mesh,
        in_specs=(
            P(("dom", "cls"), None, None),
            P("cls", None, None),
            P(),
            P(("dom", "cls")),
            P(("dom", "cls"), None),
        ),
        out_specs=P("cls", "dom", None),
        check_vma=False,
    )
```

```python
import functools

import jax
import jax.numpy as jnp
import numpy as np
from jax import lax
from jax.experimental import pallas as pl
from jax.experimental.pallas import tpu as pltpu
from jax.sharding import PartitionSpec as P

MESH = pl.DeviceIdType.MESH
VMEM = pl.BlockSpec(memory_space=pltpu.VMEM)
LIMIT = 56 * 1024 * 1024
F32 = jnp.float32
BF16 = jnp.bfloat16
EXACT = lax.Precision.HIGHEST
TILE = 16
CORES = 2


def angle_tables(angles):
    harm_count = angles // 2
    phase = np.arange(angles)[:, None] * np.arange(harm_count)[None, :] % angles
    grid = 2.0 * np.pi / angles * phase
    cosine, sine = np.cos(grid), np.sin(grid)
    forward = np.concatenate([cosine, sine], axis=1)
    weight = np.where(np.arange(harm_count) == 0, 1.0, 2.0)[:, None] / angles
    inverse = np.concatenate([cosine.T * weight, -sine.T * weight], axis=0)
    return forward.astype(np.float32), inverse.astype(np.float32)


def swap_matrix():
    rows = np.arange(TILE * TILE)
    swap = np.zeros((TILE * TILE, TILE * TILE), np.float32)
    swap[rows, rows % TILE * TILE + rows // TILE] = 1.0
    return swap


def harmonics(src, dst, swap, table, place):
    frames, cycles, angles = src.shape
    for first in range(0, cycles, TILE):
        for frame in range(0, frames, TILE):
            block = src[frame : frame + TILE, first : first + TILE, :]
            block = block.reshape(TILE * TILE, angles)
            block = jnp.dot(swap, block, preferred_element_type=F32).astype(BF16)
            out = jnp.dot(block, table, preferred_element_type=F32).astype(BF16)
            for r in range(TILE):
                chip, s = place(first + r)
                dst[chip, s, frame : frame + TILE, :] = out[r * TILE : (r + 1) * TILE]


def column(rows, index):
    lanes = lax.broadcasted_iota(jnp.int32, rows.shape, 1)
    return jnp.sum(jnp.where(lanes == index, rows, 0.0), axis=1, keepdims=True)


def class_hits(meta, priors, classes):
    lanes = lax.broadcasted_iota(jnp.int32, (meta.shape[0], classes), 1)
    return jnp.concatenate(
        [(meta[:, j : j + 1] == lanes).astype(F32) for j in range(priors)], axis=0
    )


def ctf_rows(meta, priors, table):
    groups = table.shape[0]
    lanes = lax.broadcasted_iota(jnp.int32, (meta.shape[0], groups), 1)
    hits = (meta[:, priors : priors + 1] == lanes).astype(F32)
    return jnp.dot(hits, table, precision=EXACT, preferred_element_type=F32)


def body(
    doms,
    chips,
    priors,
    deliver,
    img_ref,
    ref_ref,
    meta_ref,
    ctf_ref,
    swap_ref,
    forward_ref,
    inverse_ref,
    *rest,
):
    if deliver:
        out_ref, rest = rest[0], rest[1:]
    else:
        sum_out, norm_out, rest = rest[0], rest[1], rest[2:]
    (
        part_send,
        part_got,
        cls_send,
        cls_got,
        meta_got,
        scaled,
        ctf_got,
        score_send,
        score_got,
        spec_send,
        spec_got,
        sums,
        norms,
        half_send,
        half_got,
        half_norm,
        half_norm_got,
        sum_send,
        sum_got,
        norm_send,
        norm_got,
        low,
        high,
        cls_sem,
        pass_sem,
        meta_sem,
        part_sem,
        score_sem,
        spec_sem,
        half_sem,
        sum_sem,
        norm_sem,
    ) = rest
    dom, me = lax.axis_index("dom"), lax.axis_index("cls")
    chip, core = me // CORES, me % CORES
    sibling = (dom, me + 1 - 2 * core)
    particles, cycles, angles = img_ref.shape
    owned = ref_ref.shape[0]
    owners = chips * CORES
    classes = owners * owned
    share = cycles // chips
    harm = angles // 2
    width = 2 * harm
    held = cycles // doms
    run = max(held // owners, 1)

    def place(r):
        if not deliver:
            return r // share, r % share
        to, chip, half, one = r // held, r % held // (CORES * run), r // run % CORES, r % run
        return chip, (half * doms + to) * run + one

    places = {place(r): r for r in range(cycles)}
    first_cycle = [places[0, s] for s in range(share)]
    chip_step = places[1, 0] - places[0, 0]

    barrier = pltpu.get_barrier_semaphore()
    offsets = [(a, b) for a in range(doms if deliver else 1) for b in range(owners)][1:]

    def peer(a, b):
        return (lax.rem(dom + a, doms), lax.rem(me + b, owners))

    def chip_at(off):
        return lax.rem(chip + off + chips, chips)

    def remote(src, dst, sem, at, device):
        return pltpu.make_async_remote_copy(
            src_ref=src,
            dst_ref=dst,
            send_sem=sem.at[(0,) + at],
            recv_sem=sem.at[(1,) + at],
            device_id=device,
            device_id_type=MESH,
        )

    def same_core(off):
        return (dom, chip_at(off) * CORES + core)

    def cls_copy(off):
        return remote(cls_send.at[chip_at(off)], cls_got.at[me], cls_sem, (off,), same_core(off))

    def pass_copy(off):
        slot = cls_got.at[chip_at(-off) * CORES + core]
        return remote(slot, slot, pass_sem, (off,), sibling)

    def pass_got(off):
        slot = cls_got.at[chip_at(-off) * CORES + 1 - core]
        return remote(slot, slot, pass_sem, (off,), sibling)

    def meta_copy(off):
        return remote(meta_ref, meta_got.at[chip], meta_sem, (off,), same_core(off))

    def part_copy(off):
        return remote(
            part_send.at[chip_at(off)], part_got.at[chip], part_sem, (off,), same_core(off)
        )

    def score_copy(off):
        return remote(
            score_send.at[chip_at(-off)], score_got.at[chip], score_sem, (off,), same_core(-off)
        )

    def spec_copy(off):
        return remote(spec_send, spec_got.at[chip], spec_sem, (off,), same_core(off))

    for a, b in offsets:
        pl.semaphore_signal(barrier, inc=1, device_id=peer(a, b), device_id_type=MESH)
    table = forward_ref[...].astype(BF16)
    swap = swap_ref[...]
    harmonics(ref_ref, cls_send, swap, table, place)
    cls_got[me] = cls_send[chip]
    pl.semaphore_wait(barrier, len(offsets))
    for off in range(1, chips):
        meta_copy(off).start()
        cls_copy(off).start()
    pass_copy(0).start()
    harmonics(img_ref, part_send, swap, table, place)
    for off in range(1, chips):
        part_copy(off).start()
    part_got[chip] = part_send[chip]
    meta_got[chip] = meta_ref[...]

    def score(src):
        meta = meta_got[src]
        ctf = ctf_rows(meta, priors, ctf_ref[...])
        ctf_got[src] = ctf
        hits = class_hits(meta, priors, classes).astype(BF16)
        real, imag = 0.0, 0.0
        for s in range(share):
            part = part_got[src, s].astype(F32) * column(ctf, first_cycle[s] + chip_step * chip)
            scaled[src, s] = part
            table = cls_got[:, s].reshape(classes, width)
            picked = jnp.dot(hits, table, preferred_element_type=F32)
            picked = picked.reshape(priors, particles, width)
            pc, ps = part[None, :, :harm], part[None, :, harm:]
            cc, cs = picked[:, :, :harm], picked[:, :, harm:]
            real = real + (pc * cc + ps * cs)
            imag = imag + (pc * cs - ps * cc)
        score_send[src, :, :, :harm] = real.astype(BF16)
        score_send[src, :, :, harm:] = imag.astype(BF16)

    for off in range(1, chips):
        meta_copy(off).wait()
        cls_copy(off).wait()
        pass_copy(off).start()
    for off in range(chips):
        pass_copy(off).wait_send()
        pass_got(off).wait_recv()

    score(chip)

    @pl.loop(1, chips)
    def _(off):
        part_copy(off).wait_recv()
        score(chip_at(-off))
        score_copy(off).start()

    joined = score_send[chip].astype(F32)
    for off in range(1, chips):
        score_copy(off).wait_recv()
        joined = joined + score_got[chip_at(off)].astype(F32)
    joined = joined.reshape(priors * particles, width)
    scores = jnp.dot(joined, inverse_ref[...], precision=EXACT, preferred_element_type=F32)
    scores = scores.reshape(priors, particles, angles)
    highest = jnp.max(jnp.max(scores, axis=0), axis=1, keepdims=True)
    total = jnp.sum(jnp.sum(jnp.exp(scores - highest[None]), axis=0), axis=1, keepdims=True)
    log_total = highest + jnp.log(total)
    weights = jnp.exp(scores - log_total[None]).reshape(priors * particles, angles)
    spectrum = jnp.dot(weights, forward_ref[...], precision=EXACT, preferred_element_type=F32)
    spec_send[...] = spectrum.astype(BF16).reshape(spec_send.shape)
    for off in range(1, chips):
        spec_copy(off).start()
    spec_got[chip] = spec_send[...]
    sums[...] = jnp.zeros_like(sums)
    norms[...] = jnp.zeros_like(norms)

    def add(src):
        hits = class_hits(meta_got[src], priors, classes).T
        spectrum = spec_got[src].astype(F32)
        wc, ws = spectrum[:, :, :harm], spectrum[:, :, harm:]
        ctf = ctf_got[src]
        square = (ctf * ctf)[None] * wc[:, :, :1]
        norms[...] += jnp.dot(
            hits,
            square.reshape(priors * particles, cycles),
            precision=EXACT,
            preferred_element_type=F32,
        )
        hits = hits.astype(BF16)
        for s in range(share):
            part = scaled[src, s][None]
            pc, ps = part[:, :, :harm], part[:, :, harm:]
            terms = jnp.concatenate([pc * wc + ps * ws, ps * wc - pc * ws], axis=2)
            terms = terms.reshape(priors * particles, width).astype(BF16)
            sums[s] += jnp.dot(hits, terms, preferred_element_type=F32)

    add(chip)

    @pl.loop(1, chips)
    def _(off):
        spec_copy(off).wait_recv()
        add(chip_at(-off))

    for off in range(1, chips):
        part_copy(off).wait_send()
        score_copy(off).wait_send()
        spec_copy(off).wait_send()

    if not deliver:
        sum_out[...] = sums[...].astype(BF16)
        norm_out[...] = norms[...]
        return

    half = doms * run
    mine = pl.multiple_of(me * owned, owned)
    other = pl.multiple_of(sibling[1] * owned, owned)
    half_send[...] = sums[pl.ds((1 - core) * half, half)].astype(BF16)
    half_norm[:, :cycles] = norms[pl.ds(other, owned), :]
    sum_half = remote(half_send, half_got, half_sem, (0,), sibling)
    norm_half = remote(half_norm, half_norm_got, half_sem, (1,), sibling)
    sum_half.start()
    norm_half.start()
    sum_half.wait()
    norm_half.wait()
    norm_send[:, :cycles] = norms[pl.ds(mine, owned), :] + half_norm_got[:, :cycles]

    def sum_copy(a, b):
        to = peer(a, b)
        start = pl.multiple_of(to[1] * owned, owned)
        src = sum_send.at[pl.ds(to[0] * run, run), pl.ds(start, owned), :]
        return remote(src, sum_got.at[dom, me], sum_sem, (a, b), to)

    def norm_copy(a):
        return remote(norm_send, norm_got.at[dom], norm_sem, (a,), peer(a, 0))

    for a in sorted(range(doms), key=lambda a: (a == 0, abs(a - doms // 2))):
        at = pl.ds(peer(a, 0)[0] * run, run)
        own = sums[pl.ds(core * half + peer(a, 0)[0] * run, run)]
        sum_send[at] = (own + half_got[at].astype(F32)).astype(BF16)
        for b in range(owners):
            if (a, b) in offsets:
                sum_copy(a, b).start()
        if a:
            norm_copy(a).start()
    sum_got[dom, me] = sum_send[pl.ds(dom * run, run), pl.ds(mine, owned), :]
    norm_got[dom] = norm_send[...]
    for a, b in offsets:
        sum_copy(a, b).wait()
    for a in range(1, doms):
        norm_copy(a).wait()
    total_norm = norm_got[0, :, :cycles]
    for a in range(1, doms):
        total_norm = total_norm + norm_got[a, :, :cycles]
    for c in range(owners):
        for one in range(run):
            cycle = c * run + one
            result = sum_got[0, c, one].astype(F32)
            for a in range(1, doms):
                result = result + sum_got[a, c, one].astype(F32)
            result = result / (column(total_norm, dom * held + cycle) + 1.0)
            at = pl.ds(cycle, owned, stride=held)
            low[at, :] = result[:, :harm]
            high[at, :] = result[:, harm:]
    out_ref[:, :harm] = low[...]
    out_ref[:, harm:] = high[...]


def on_device(doms, images, references, ctf_table, defocus, priors):
    owners = lax.axis_size("cls")
    particles, cycles, angles = images.shape
    owned = references.shape[0]
    classes = owners * owned
    prior_count = priors.shape[1]
    chips = owners // CORES
    share = cycles // chips
    width = angles // 2 * 2
    held = cycles // doms
    deliver = held % owners == 0
    run = max(held // owners, 1)
    forward, inverse = (jnp.asarray(t) for t in angle_tables(angles))
    swap = jnp.asarray(swap_matrix(), BF16)
    meta = jnp.concatenate(
        [priors, defocus[:, None], jnp.zeros((particles, 127 - prior_count), jnp.int32)], axis=1
    )
    if deliver:
        shapes = [jax.ShapeDtypeStruct((owned * held, width), F32)]
    else:
        shapes = [
            jax.ShapeDtypeStruct((share, classes, width), BF16),
            jax.ShapeDtypeStruct((classes, cycles), F32),
        ]
    slots = (prior_count, particles, width)
    sums = (share, classes, width)
    half = (doms * run, classes, width)
    pair_sem = pltpu.SemaphoreType.DMA((2, chips))
    done = pl.pallas_call(
        functools.partial(body, doms, chips, prior_count, deliver),
        out_shape=shapes,
        in_specs=[VMEM] * 7,
        out_specs=[VMEM] * len(shapes),
        scratch_shapes=[
            pltpu.VMEM((chips, share, particles, width), BF16),
            pltpu.VMEM((chips, share, particles, width), BF16),
            pltpu.VMEM((chips, share, owned, width), BF16),
            pltpu.VMEM((owners, share, owned, width), BF16),
            pltpu.VMEM((chips,) + meta.shape, jnp.int32),
            pltpu.VMEM((chips, share, particles, width), F32),
            pltpu.VMEM((chips, particles, cycles), F32),
            pltpu.VMEM((chips,) + slots, BF16),
            pltpu.VMEM((chips,) + slots, BF16),
            pltpu.VMEM(slots, BF16),
            pltpu.VMEM((chips,) + slots, BF16),
            pltpu.VMEM(sums, F32),
            pltpu.VMEM((classes, cycles), F32),
            pltpu.VMEM(half, BF16),
            pltpu.VMEM(half, BF16),
            pltpu.VMEM((owned, 128), F32),
            pltpu.VMEM((owned, 128), F32),
            pltpu.VMEM(half, BF16),
            pltpu.VMEM((doms, owners, run, owned, width), BF16),
            pltpu.VMEM((owned, 128), F32),
            pltpu.VMEM((doms, owned, 128), F32),
            pltpu.VMEM((owned * held, width // 2), F32),
            pltpu.VMEM((owned * held, width // 2), F32),
            pair_sem,
            pair_sem,
            pair_sem,
            pair_sem,
            pair_sem,
            pair_sem,
            pltpu.SemaphoreType.DMA((2, 2)),
            pltpu.SemaphoreType.DMA((2, doms, owners)),
            pltpu.SemaphoreType.DMA((2, doms)),
        ],
        compiler_params=pltpu.CompilerParams(
            collective_id=1, has_side_effects=True, vmem_limit_bytes=LIMIT
        ),
    )(images, references, meta, ctf_table, swap, forward, inverse)
    if deliver:
        return done[0].reshape(owned, held, width)
    sums, norms = done
    me = lax.axis_index("cls")
    chip, core = me // CORES, me % CORES
    mine = chip * share + jnp.arange(share)
    placed = jnp.zeros((cycles, classes, width), F32).at[mine].set(sums.astype(F32))
    placed = lax.psum_scatter(placed, "dom", scatter_dimension=0, tiled=True)
    placed = lax.psum_scatter(placed, "cls", scatter_dimension=1, tiled=True)
    rows = jnp.arange(classes)[:, None] // (CORES * owned)
    norms = jnp.where(rows == chip, norms, 0.0)
    norms = lax.psum_scatter(norms, "dom", scatter_dimension=1, tiled=True)
    norms = lax.psum_scatter(norms, "cls", scatter_dimension=0, tiled=True)
    return placed.transpose(1, 0, 2) / (norms + 1.0)[:, :, None]


def solution(mesh):
    return jax.shard_map(
        functools.partial(on_device, mesh.shape["dom"]),
        mesh=mesh,
        in_specs=(
            P(("dom", "cls"), None, None),
            P("cls", None, None),
            P(),
            P(("dom", "cls")),
            P(("dom", "cls"), None),
        ),
        out_specs=P("cls", "dom", None),
        check_vma=False,
    )
```

```python
import functools

import jax
import jax.numpy as jnp
import numpy as np
from jax import lax
from jax.experimental import pallas as pl
from jax.experimental.pallas import tpu as pltpu
from jax.sharding import PartitionSpec as P

MESH = pl.DeviceIdType.MESH
VMEM = pl.BlockSpec(memory_space=pltpu.VMEM)
LIMIT = 56 * 1024 * 1024
F32 = jnp.float32
BF16 = jnp.bfloat16
EXACT = lax.Precision.HIGHEST
TILE = 16
CORES = 2
BATCHES = 2


def angle_tables(angles):
    harm_count = angles // 2
    phase = np.arange(angles)[:, None] * np.arange(harm_count)[None, :] % angles
    grid = 2.0 * np.pi / angles * phase
    cosine, sine = np.cos(grid), np.sin(grid)
    forward = np.concatenate([cosine, sine], axis=1)
    weight = np.where(np.arange(harm_count) == 0, 1.0, 2.0)[:, None] / angles
    inverse = np.concatenate([cosine.T * weight, -sine.T * weight], axis=0)
    return forward.astype(np.float32), inverse.astype(np.float32)


def swap_matrix():
    rows = np.arange(TILE * TILE)
    swap = np.zeros((TILE * TILE, TILE * TILE), np.float32)
    swap[rows, rows % TILE * TILE + rows // TILE] = 1.0
    return swap


def harmonics(src, dst, swap, table, place):
    frames, cycles, angles = src.shape
    for first in range(0, cycles, TILE):
        for frame in range(0, frames, TILE):
            block = src[frame : frame + TILE, first : first + TILE, :]
            block = block.reshape(TILE * TILE, angles)
            block = jnp.dot(swap, block, preferred_element_type=F32).astype(BF16)
            out = jnp.dot(block, table, preferred_element_type=F32).astype(BF16)
            for r in range(TILE):
                chip, s = place(first + r)
                dst[chip, s, frame : frame + TILE, :] = out[r * TILE : (r + 1) * TILE]


def column(rows, index):
    lanes = lax.broadcasted_iota(jnp.int32, rows.shape, 1)
    return jnp.sum(jnp.where(lanes == index, rows, 0.0), axis=1, keepdims=True)


def class_hits(meta, priors, classes):
    lanes = lax.broadcasted_iota(jnp.int32, (meta.shape[0], classes), 1)
    return jnp.concatenate(
        [(meta[:, j : j + 1] == lanes).astype(F32) for j in range(priors)], axis=0
    )


def split(rows):
    high = rows.astype(BF16)
    return high, (rows - high.astype(F32)).astype(BF16)


def table_product(rows, table):
    high, low = split(rows)
    table_high, table_low = split(table)
    total = jnp.dot(high, table_low, preferred_element_type=F32)
    total = total + jnp.dot(low, table_high, preferred_element_type=F32)
    return total + jnp.dot(high, table_high, preferred_element_type=F32)


def ctf_rows(meta, priors, table):
    groups = table.shape[0]
    lanes = lax.broadcasted_iota(jnp.int32, (meta.shape[0], groups), 1)
    hits = (meta[:, priors : priors + 1] == lanes).astype(F32)
    return jnp.dot(hits, table, precision=EXACT, preferred_element_type=F32)


def body(
    doms,
    chips,
    priors,
    deliver,
    img_ref,
    ref_ref,
    meta_ref,
    ctf_ref,
    swap_ref,
    forward_ref,
    inverse_ref,
    *rest,
):
    if deliver:
        out_ref, rest = rest[0], rest[1:]
    else:
        sum_out, norm_out, rest = rest[0], rest[1], rest[2:]
    (
        img_got,
        part_send,
        part_got,
        cls_send,
        cls_got,
        meta_got,
        scaled,
        ctf_got,
        hits,
        hits_t,
        terms,
        score_send,
        score_got,
        spec_send,
        spec_got,
        sums,
        norms,
        half_send,
        half_got,
        half_norm,
        half_norm_got,
        sum_send,
        sum_got,
        norm_send,
        norm_got,
        low,
        high,
        img_sem,
        cls_sem,
        pass_sem,
        meta_sem,
        part_sem,
        score_sem,
        spec_sem,
        half_sem,
        sum_sem,
        norm_sem,
    ) = rest
    dom, me = lax.axis_index("dom"), lax.axis_index("cls")
    chip, core = me // CORES, me % CORES
    sibling = (dom, me + 1 - 2 * core)
    particles, cycles, angles = img_ref.shape
    batch = particles // BATCHES
    slots = priors * batch
    owned = ref_ref.shape[0]
    owners = chips * CORES
    classes = owners * owned
    share = cycles // chips
    harm = angles // 2
    width = 2 * harm
    held = cycles // doms
    run = max(held // owners, 1)

    def place(r):
        if not deliver:
            return r // share, r % share
        to, chip, half, one = r // held, r % held // (CORES * run), r // run % CORES, r % run
        return chip, (half * doms + to) * run + one

    places = {place(r): r for r in range(cycles)}
    first_cycle = [places[0, s] for s in range(share)]
    chip_step = places[1, 0] - places[0, 0]

    barrier = pltpu.get_barrier_semaphore()
    offsets = [(a, b) for a in range(doms if deliver else 1) for b in range(owners)][1:]

    def peer(a, b):
        return (lax.rem(dom + a, doms), lax.rem(me + b, owners))

    def chip_at(off):
        return lax.rem(chip + off + chips, chips)

    def remote(src, dst, sem, at, device):
        return pltpu.make_async_remote_copy(
            src_ref=src,
            dst_ref=dst,
            send_sem=sem.at[(0,) + at],
            recv_sem=sem.at[(1,) + at],
            device_id=device,
            device_id_type=MESH,
        )

    def same_core(off):
        return (dom, chip_at(off) * CORES + core)

    def cls_copy(off):
        return remote(cls_send.at[chip_at(off)], cls_got.at[me], cls_sem, (off,), same_core(off))

    def pass_copy(off):
        slot = cls_got.at[chip_at(-off) * CORES + core]
        return remote(slot, slot, pass_sem, (off,), sibling)

    def pass_got(off):
        slot = cls_got.at[chip_at(-off) * CORES + 1 - core]
        return remote(slot, slot, pass_sem, (off,), sibling)

    def meta_copy(off):
        return remote(meta_ref, meta_got.at[chip], meta_sem, (off,), same_core(off))

    def frames_of(b):
        return pl.ds(b * batch, batch)

    def part_copy(off, b):
        return remote(
            part_send.at[chip_at(off), :, frames_of(b), :],
            part_got.at[chip, :, frames_of(b), :],
            part_sem,
            (off, b),
            same_core(off),
        )

    def score_copy(off, b):
        return remote(
            score_send.at[chip_at(-off), b],
            score_got.at[chip, b],
            score_sem,
            (off, b),
            same_core(-off),
        )

    def spec_copy(off, b):
        return remote(spec_send.at[b], spec_got.at[chip, b], spec_sem, (off, b), same_core(off))

    images = pltpu.make_async_copy(img_ref, img_got, img_sem)
    images.start()
    for a, b in offsets:
        pl.semaphore_signal(barrier, inc=1, device_id=peer(a, b), device_id_type=MESH)
    table = forward_ref[...].astype(BF16)
    swap = swap_ref[...]
    harmonics(ref_ref, cls_send, swap, table, place)
    cls_got[me] = cls_send[chip]
    pl.semaphore_wait(barrier, len(offsets))
    for off in range(1, chips):
        meta_copy(off).start()
        cls_copy(off).start()
    pass_copy(0).start()
    images.wait()
    harmonics(img_got, part_send, swap, table, place)
    for b in range(BATCHES):
        for off in range(1, chips):
            part_copy(off, b).start()
    part_got[chip] = part_send[chip]
    meta_got[chip] = meta_ref[...]
    sums[...] = jnp.zeros_like(sums)
    norms[...] = jnp.zeros_like(norms)
    for off in range(1, chips):
        meta_copy(off).wait()

    def lanes_of(src, b):
        return pl.ds(pl.multiple_of((src * BATCHES + b) * slots, slots), slots)

    @pl.loop(0, chips)
    def _(src):
        ctf_got[src] = ctf_rows(meta_got[src], priors, ctf_ref[...])
        for b in range(BATCHES):
            found = class_hits(meta_got[src, frames_of(b)], priors, classes)
            hits[src, b] = found.astype(BF16)
            hits_t[:, lanes_of(src, b)] = found.T.astype(BF16)

    for off in range(1, chips):
        cls_copy(off).wait()
        pass_copy(off).start()
    for off in range(chips):
        pass_copy(off).wait_send()
        pass_got(off).wait_recv()

    def score(src, b):
        ctf = ctf_got[src, frames_of(b)]
        real, imag = 0.0, 0.0
        for s in range(share):
            part = part_got[src, s, frames_of(b)].astype(F32)
            part = part * column(ctf, first_cycle[s] + chip_step * chip)
            scaled[src, s, frames_of(b)] = part
            table = cls_got[:, s].reshape(classes, width)
            picked = jnp.dot(hits[src, b], table, preferred_element_type=F32)
            picked = picked.reshape(priors, batch, width)
            pc, ps = part[None, :, :harm], part[None, :, harm:]
            cc, cs = picked[:, :, :harm], picked[:, :, harm:]
            real = real + (pc * cc + ps * cs)
            imag = imag + (pc * cs - ps * cc)
        score_send[src, b, :, :, :harm] = real.astype(BF16)
        score_send[src, b, :, :, harm:] = imag.astype(BF16)

    for b in range(BATCHES):
        score(chip, b)
    for b in range(BATCHES):

        @pl.loop(1, chips)
        def _(off):
            part_copy(off, b).wait_recv()
            score(chip_at(-off), b)
            score_copy(off, b).start()

    for b in range(BATCHES):
        joined = score_send[chip, b].astype(F32)
        for off in range(1, chips):
            score_copy(off, b).wait_recv()
            joined = joined + score_got[chip_at(off), b].astype(F32)
        scores = table_product(joined.reshape(slots, width), inverse_ref[...])
        scores = scores.reshape(priors, batch, angles)
        highest = jnp.max(jnp.max(scores, axis=0), axis=1, keepdims=True)
        total = jnp.sum(jnp.exp(scores - highest[None]), axis=0)
        log_total = highest + jnp.log(jnp.sum(total, axis=1, keepdims=True))
        weights = jnp.exp(scores - log_total[None]).reshape(slots, angles)
        spectrum = table_product(weights, forward_ref[...])
        spec_send[b] = spectrum.astype(BF16).reshape(priors, batch, width)
        for off in range(1, chips):
            spec_copy(off, b).start()
        spec_got[chip, b] = spec_send[b]

    half = doms * run
    other_half, own_half = ((1 - core) * half, core * half) if deliver else (0, 0)

    def slot_terms(src, b, s):
        spectrum = spec_got[src, b].astype(F32)
        wc, ws = spectrum[:, :, :harm], spectrum[:, :, harm:]
        part = scaled[src, s, frames_of(b)][None]
        pc, ps = part[:, :, :harm], part[:, :, harm:]
        both = jnp.concatenate([pc * wc + ps * ws, ps * wc - pc * ws], axis=2)
        return both.reshape(slots, width).astype(BF16)

    def add(src, b):
        chosen = hits_t[:, lanes_of(src, b)]
        ctf = ctf_got[src, frames_of(b)]
        square = (ctf * ctf)[None] * spec_got[src, b, :, :, :1].astype(F32)
        parts = jnp.concatenate(split(square.reshape(slots, cycles)), axis=1)
        norms[...] += jnp.dot(chosen, parts, preferred_element_type=F32)
        for i in range(sums.shape[0]):
            sums[i] += jnp.dot(
                chosen, slot_terms(src, b, other_half + i), preferred_element_type=F32
            )

    for b in range(BATCHES):
        add(chip, b)
    for b in range(BATCHES):

        @pl.loop(1, chips)
        def _(off):
            spec_copy(off, b).wait_recv()
            add(chip_at(-off), b)

    for b in range(BATCHES):
        for off in range(1, chips):
            part_copy(off, b).wait_send()
            score_copy(off, b).wait_send()
            spec_copy(off, b).wait_send()
    norms[:, :cycles] += norms[:, cycles:]

    if not deliver:
        sum_out[...] = sums[...].astype(BF16)
        norm_out[...] = norms[:, :cycles]
        return

    mine = pl.multiple_of(me * owned, owned)
    other = pl.multiple_of(sibling[1] * owned, owned)
    half_send[...] = sums[...].astype(BF16)
    half_norm[...] = norms[pl.ds(other, owned), :]
    sum_half = remote(half_send, half_got, half_sem, (0,), sibling)
    norm_half = remote(half_norm, half_norm_got, half_sem, (1,), sibling)
    sum_half.start()
    norm_half.start()
    def sum_copy(a, b):
        to = peer(a, b)
        start = pl.multiple_of(to[1] * owned, owned)
        src = sum_send.at[pl.ds(to[0] * run, run), pl.ds(start, owned), :]
        return remote(src, sum_got.at[dom, me], sum_sem, (a, b), to)

    def norm_copy(a):
        return remote(norm_send, norm_got.at[dom], norm_sem, (a,), peer(a, 0))

    waited = False
    for a in sorted(range(doms), key=lambda a: (a == 0, abs(a - doms // 2))):
        first = peer(a, 0)[0] * run
        own = []
        for one in range(run):
            for src in range(chips):
                for b in range(BATCHES):
                    at = pl.ds((src * BATCHES + b) * slots, slots)
                    terms[one, at, :] = slot_terms(src, b, own_half + first + one)
            own.append(jnp.dot(hits_t[...], terms[one], preferred_element_type=F32))
        if not waited:
            sum_half.wait()
            norm_half.wait()
            norm_send[...] = norms[pl.ds(mine, owned), :] + half_norm_got[...]
            waited = True
        for one in range(run):
            both = own[one] + half_got[first + one].astype(F32)
            sum_send[first + one] = both.astype(BF16)
        for b in range(owners):
            if (a, b) in offsets:
                sum_copy(a, b).start()
        if a:
            norm_copy(a).start()
    sum_got[dom, me] = sum_send[pl.ds(dom * run, run), pl.ds(mine, owned), :]
    norm_got[dom] = norm_send[...]
    for a, b in offsets:
        sum_copy(a, b).wait()
    for a in range(1, doms):
        norm_copy(a).wait()
    total_norm = norm_got[0, :, :cycles]
    for a in range(1, doms):
        total_norm = total_norm + norm_got[a, :, :cycles]
    for c in range(owners):
        for one in range(run):
            cycle = c * run + one
            result = sum_got[0, c, one].astype(F32)
            for a in range(1, doms):
                result = result + sum_got[a, c, one].astype(F32)
            result = result / (column(total_norm, dom * held + cycle) + 1.0)
            at = pl.ds(cycle, owned, stride=held)
            low[at, :] = result[:, :harm]
            high[at, :] = result[:, harm:]
    out_ref[:, :harm] = low[...]
    out_ref[:, harm:] = high[...]


def on_device(doms, images, references, ctf_table, defocus, priors):
    owners = lax.axis_size("cls")
    particles, cycles, angles = images.shape
    owned = references.shape[0]
    classes = owners * owned
    prior_count = priors.shape[1]
    chips = owners // CORES
    share = cycles // chips
    width = angles // 2 * 2
    held = cycles // doms
    deliver = held % owners == 0
    run = max(held // owners, 1)
    forward, inverse = (jnp.asarray(t) for t in angle_tables(angles))
    swap = jnp.asarray(swap_matrix(), BF16)
    meta = jnp.concatenate(
        [priors, defocus[:, None], jnp.zeros((particles, 127 - prior_count), jnp.int32)], axis=1
    )
    if deliver:
        shapes = [jax.ShapeDtypeStruct((owned * held, width), F32)]
    else:
        shapes = [
            jax.ShapeDtypeStruct((share, classes, width), BF16),
            jax.ShapeDtypeStruct((classes, cycles), F32),
        ]
    batch = particles // BATCHES
    slots = (BATCHES, prior_count, batch, width)
    rows = prior_count * batch
    sums = (share, classes, width)
    half = (doms * run, classes, width)
    pair_sem = pltpu.SemaphoreType.DMA((2, chips))
    batch_sem = pltpu.SemaphoreType.DMA((2, chips, BATCHES))
    done = pl.pallas_call(
        functools.partial(body, doms, chips, prior_count, deliver),
        out_shape=shapes,
        in_specs=[pl.BlockSpec(memory_space=pl.ANY)] + [VMEM] * 6,
        out_specs=[VMEM] * len(shapes),
        scratch_shapes=[
            pltpu.VMEM(images.shape, BF16),
            pltpu.VMEM((chips, share, particles, width), BF16),
            pltpu.VMEM((chips, share, particles, width), BF16),
            pltpu.VMEM((chips, share, owned, width), BF16),
            pltpu.VMEM((owners, share, owned, width), BF16),
            pltpu.VMEM((chips,) + meta.shape, jnp.int32),
            pltpu.VMEM((chips, share, particles, width), F32),
            pltpu.VMEM((chips, particles, cycles), F32),
            pltpu.VMEM((chips, BATCHES, rows, classes), BF16),
            pltpu.VMEM((classes, chips * BATCHES * rows), BF16),
            pltpu.VMEM((run, chips * BATCHES * rows, width), BF16),
            pltpu.VMEM((chips,) + slots, BF16),
            pltpu.VMEM((chips,) + slots, BF16),
            pltpu.VMEM(slots, BF16),
            pltpu.VMEM((chips,) + slots, BF16),
            pltpu.VMEM(half if deliver else sums, F32),
            pltpu.VMEM((classes, 2 * cycles), F32),
            pltpu.VMEM(half, BF16),
            pltpu.VMEM(half, BF16),
            pltpu.VMEM((owned, 2 * cycles), F32),
            pltpu.VMEM((owned, 2 * cycles), F32),
            pltpu.VMEM(half, BF16),
            pltpu.VMEM((doms, owners, run, owned, width), BF16),
            pltpu.VMEM((owned, 2 * cycles), F32),
            pltpu.VMEM((doms, owned, 2 * cycles), F32),
            pltpu.VMEM((owned * held, width // 2), F32),
            pltpu.VMEM((owned * held, width // 2), F32),
            pltpu.SemaphoreType.DMA,
            pair_sem,
            pair_sem,
            pair_sem,
            batch_sem,
            batch_sem,
            batch_sem,
            pltpu.SemaphoreType.DMA((2, 2)),
            pltpu.SemaphoreType.DMA((2, doms, owners)),
            pltpu.SemaphoreType.DMA((2, doms)),
        ],
        compiler_params=pltpu.CompilerParams(
            collective_id=1, has_side_effects=True, vmem_limit_bytes=LIMIT
        ),
    )(images, references, meta, ctf_table, swap, forward, inverse)
    if deliver:
        return done[0].reshape(owned, held, width)
    sums, norms = done
    me = lax.axis_index("cls")
    chip = me // CORES
    mine = chip * share + jnp.arange(share)
    placed = jnp.zeros((cycles, classes, width), F32).at[mine].set(sums.astype(F32))
    placed = lax.psum_scatter(placed, "dom", scatter_dimension=0, tiled=True)
    placed = lax.psum_scatter(placed, "cls", scatter_dimension=1, tiled=True)
    rows = jnp.arange(classes)[:, None] // (CORES * owned)
    norms = jnp.where(rows == chip, norms, 0.0)
    norms = lax.psum_scatter(norms, "dom", scatter_dimension=1, tiled=True)
    norms = lax.psum_scatter(norms, "cls", scatter_dimension=0, tiled=True)
    return placed.transpose(1, 0, 2) / (norms + 1.0)[:, :, None]


def solution(mesh):
    return jax.shard_map(
        functools.partial(on_device, mesh.shape["dom"]),
        mesh=mesh,
        in_specs=(
            P(("dom", "cls"), None, None),
            P("cls", None, None),
            P(),
            P(("dom", "cls")),
            P(("dom", "cls"), None),
        ),
        out_specs=P("cls", "dom", None),
        check_vma=False,
    )
```

```python
import functools

import jax
import jax.numpy as jnp
import numpy as np
from jax import lax
from jax.experimental import pallas as pl
from jax.experimental.pallas import tpu as pltpu
from jax.sharding import PartitionSpec as P

MESH = pl.DeviceIdType.MESH
VMEM = pl.BlockSpec(memory_space=pltpu.VMEM)
LIMIT = 56 * 1024 * 1024
F32 = jnp.float32
BF16 = jnp.bfloat16
EXACT = lax.Precision.HIGHEST
TILE = 16
CORES = 2
BATCHES = 2


def angle_tables(angles):
    harm_count = angles // 2
    phase = np.arange(angles)[:, None] * np.arange(harm_count)[None, :] % angles
    grid = 2.0 * np.pi / angles * phase
    cosine, sine = np.cos(grid), np.sin(grid)
    forward = np.concatenate([cosine, sine], axis=1)
    weight = np.where(np.arange(harm_count) == 0, 1.0, 2.0)[:, None] / angles
    inverse = np.concatenate([cosine.T * weight, -sine.T * weight], axis=0)
    return forward.astype(np.float32), inverse.astype(np.float32)


def swap_matrix():
    rows = np.arange(TILE * TILE)
    swap = np.zeros((TILE * TILE, TILE * TILE), np.float32)
    swap[rows, rows % TILE * TILE + rows // TILE] = 1.0
    return swap


def harmonics(src, dst, swap, table, place):
    frames, cycles, angles = src.shape
    for first in range(0, cycles, TILE):
        for frame in range(0, frames, TILE):
            block = src[frame : frame + TILE, first : first + TILE, :]
            block = block.reshape(TILE * TILE, angles)
            block = jnp.dot(swap, block, preferred_element_type=F32).astype(BF16)
            out = jnp.dot(block, table, preferred_element_type=F32).astype(BF16)
            for r in range(TILE):
                chip, s = place(first + r)
                dst[chip, s, frame : frame + TILE, :] = out[r * TILE : (r + 1) * TILE]


def column(rows, index):
    lanes = lax.broadcasted_iota(jnp.int32, rows.shape, 1)
    return jnp.sum(jnp.where(lanes == index, rows, 0.0), axis=1, keepdims=True)


def class_hits(meta, priors, classes):
    lanes = lax.broadcasted_iota(jnp.int32, (meta.shape[0], classes), 1)
    return jnp.concatenate(
        [(meta[:, j : j + 1] == lanes).astype(F32) for j in range(priors)], axis=0
    )


def split(rows):
    high = rows.astype(BF16)
    return high, (rows - high.astype(F32)).astype(BF16)


def table_product(rows, table):
    high, low = split(rows)
    table_high, table_low = split(table)
    total = jnp.dot(high, table_low, preferred_element_type=F32)
    total = total + jnp.dot(low, table_high, preferred_element_type=F32)
    return total + jnp.dot(high, table_high, preferred_element_type=F32)


def ctf_rows(meta, priors, table):
    groups = table.shape[0]
    lanes = lax.broadcasted_iota(jnp.int32, (meta.shape[0], groups), 1)
    hits = (meta[:, priors : priors + 1] == lanes).astype(F32)
    return jnp.dot(hits, table, precision=EXACT, preferred_element_type=F32)


def body(
    doms,
    chips,
    priors,
    deliver,
    img_ref,
    ref_ref,
    priors_ref,
    defocus_ref,
    ctf_ref,
    swap_ref,
    forward_ref,
    inverse_ref,
    *rest,
):
    if deliver:
        sum_got, norm_got, rest = rest[0], rest[1], rest[2:]
    else:
        sum_out, norm_out, rest = rest[0], rest[1], rest[2:]
    (
        img_got,
        part_send,
        part_got,
        cls_send,
        cls_got,
        meta_send,
        meta_got,
        scaled,
        ctf_got,
        hits,
        hits_t,
        terms,
        score_send,
        score_got,
        spec_send,
        spec_got,
        sums,
        norms,
        half_send,
        half_got,
        half_norm,
        half_norm_got,
        sum_send,
        norm_send,
        img_sem,
        cls_sem,
        pass_sem,
        meta_sem,
        part_sem,
        score_sem,
        spec_sem,
        half_sem,
        sum_sem,
        norm_sem,
    ) = rest
    dom, me = lax.axis_index("dom"), lax.axis_index("cls")
    chip, core = me // CORES, me % CORES
    sibling = (dom, me + 1 - 2 * core)
    particles, cycles, angles = img_ref.shape
    batch = particles // BATCHES
    slots = priors * batch
    owned = ref_ref.shape[0]
    owners = chips * CORES
    classes = owners * owned
    share = cycles // chips
    harm = angles // 2
    width = 2 * harm
    held = cycles // doms
    run = max(held // owners, 1)

    def place(r):
        if not deliver:
            return r // share, r % share
        to, chip, half, one = r // held, r % held // (CORES * run), r // run % CORES, r % run
        return chip, (half * doms + to) * run + one

    places = {place(r): r for r in range(cycles)}
    first_cycle = [places[0, s] for s in range(share)]
    chip_step = places[1, 0] - places[0, 0]

    barrier = pltpu.get_barrier_semaphore()
    offsets = [(a, b) for a in range(doms if deliver else 1) for b in range(owners)][1:]

    def peer(a, b):
        return (lax.rem(dom + a, doms), lax.rem(me + b, owners))

    def chip_at(off):
        return lax.rem(chip + off + chips, chips)

    def remote(src, dst, sem, at, device):
        return pltpu.make_async_remote_copy(
            src_ref=src,
            dst_ref=dst,
            send_sem=sem.at[(0,) + at],
            recv_sem=sem.at[(1,) + at],
            device_id=device,
            device_id_type=MESH,
        )

    def same_core(off):
        return (dom, chip_at(off) * CORES + core)

    def cls_copy(off):
        return remote(cls_send.at[chip_at(off)], cls_got.at[me], cls_sem, (off,), same_core(off))

    def pass_copy(off):
        slot = cls_got.at[chip_at(-off) * CORES + core]
        return remote(slot, slot, pass_sem, (off,), sibling)

    def pass_got(off):
        slot = cls_got.at[chip_at(-off) * CORES + 1 - core]
        return remote(slot, slot, pass_sem, (off,), sibling)

    def meta_copy(off):
        return remote(meta_send, meta_got.at[chip], meta_sem, (off,), same_core(off))

    def frames_of(b):
        return pl.ds(b * batch, batch)

    def part_copy(off, b):
        return remote(
            part_send.at[chip_at(off), :, frames_of(b), :],
            part_got.at[chip, :, frames_of(b), :],
            part_sem,
            (off, b),
            same_core(off),
        )

    def score_copy(off, b):
        return remote(
            score_send.at[chip_at(-off), b],
            score_got.at[chip, b],
            score_sem,
            (off, b),
            same_core(-off),
        )

    def spec_copy(off, b):
        return remote(spec_send.at[b], spec_got.at[chip, b], spec_sem, (off, b), same_core(off))

    images = pltpu.make_async_copy(img_ref, img_got, img_sem)
    images.start()
    for a, b in offsets:
        pl.semaphore_signal(barrier, inc=1, device_id=peer(a, b), device_id_type=MESH)
    meta_send[...] = jnp.zeros_like(meta_send)
    meta_send[:priors, :particles] = priors_ref[...]
    meta_send[priors : priors + 1, :particles] = defocus_ref[...]
    table = forward_ref[...].astype(BF16)
    swap = swap_ref[...]
    harmonics(ref_ref, cls_send, swap, table, place)
    cls_got[me] = cls_send[chip]
    pl.semaphore_wait(barrier, len(offsets))
    for off in range(1, chips):
        meta_copy(off).start()
        cls_copy(off).start()
    pass_copy(0).start()
    images.wait()
    harmonics(img_got, part_send, swap, table, place)
    for b in range(BATCHES):
        for off in range(1, chips):
            part_copy(off, b).start()
    part_got[chip] = part_send[chip]
    meta_got[chip] = meta_send[...]
    sums[...] = jnp.zeros_like(sums)
    norms[...] = jnp.zeros_like(norms)
    for off in range(1, chips):
        meta_copy(off).wait()

    def lanes_of(src, b):
        return pl.ds(pl.multiple_of((src * BATCHES + b) * slots, slots), slots)

    @pl.loop(0, chips)
    def _(src):
        meta = meta_got[src].astype(F32).T[:particles].astype(jnp.int32)
        ctf_got[src] = ctf_rows(meta, priors, ctf_ref[...])
        for b in range(BATCHES):
            found = class_hits(meta[b * batch : (b + 1) * batch], priors, classes)
            hits[src, b] = found.astype(BF16)
            hits_t[:, lanes_of(src, b)] = found.T.astype(BF16)

    for off in range(1, chips):
        cls_copy(off).wait()
        pass_copy(off).start()
    for off in range(chips):
        pass_copy(off).wait_send()
        pass_got(off).wait_recv()

    def score(src, b):
        ctf = ctf_got[src, frames_of(b)]
        real, imag = 0.0, 0.0
        for s in range(share):
            part = part_got[src, s, frames_of(b)].astype(F32)
            part = part * column(ctf, first_cycle[s] + chip_step * chip)
            scaled[src, s, frames_of(b)] = part.astype(BF16)
            table = cls_got[:, s].reshape(classes, width)
            picked = jnp.dot(hits[src, b], table, preferred_element_type=F32)
            picked = picked.reshape(priors, batch, width)
            pc, ps = part[None, :, :harm], part[None, :, harm:]
            cc, cs = picked[:, :, :harm], picked[:, :, harm:]
            real = real + (pc * cc + ps * cs)
            imag = imag + (pc * cs - ps * cc)
        score_send[src, b, :, :, :harm] = real.astype(BF16)
        score_send[src, b, :, :, harm:] = imag.astype(BF16)

    for b in range(BATCHES):
        score(chip, b)
    for b in range(BATCHES):

        @pl.loop(1, chips)
        def _(off):
            part_copy(off, b).wait_recv()
            score(chip_at(-off), b)
            score_copy(off, b).start()

    for b in range(BATCHES):
        joined = score_send[chip, b].astype(F32)
        for off in range(1, chips):
            score_copy(off, b).wait_recv()
            joined = joined + score_got[chip_at(off), b].astype(F32)
        scores = table_product(joined.reshape(slots, width), inverse_ref[...])
        scores = scores.reshape(priors, batch, angles)
        highest = jnp.max(jnp.max(scores, axis=0), axis=1, keepdims=True)
        total = jnp.sum(jnp.exp(scores - highest[None]), axis=0)
        log_total = highest + jnp.log(jnp.sum(total, axis=1, keepdims=True))
        weights = jnp.exp(scores - log_total[None]).reshape(slots, angles)
        spectrum = table_product(weights, forward_ref[...])
        spec_send[b] = spectrum.astype(BF16).reshape(priors, batch, width)
        for off in range(1, chips):
            spec_copy(off, b).start()
        spec_got[chip, b] = spec_send[b]

    half = doms * run
    other_half, own_half = ((1 - core) * half, core * half) if deliver else (0, 0)

    def slot_terms(src, b, s):
        spectrum = spec_got[src, b]
        wc, ws = spectrum[:, :, :harm], spectrum[:, :, harm:]
        part = scaled[src, s, frames_of(b)][None]
        pc, ps = part[:, :, :harm], part[:, :, harm:]
        both = jnp.concatenate([pc * wc + ps * ws, ps * wc - pc * ws], axis=2)
        return both.reshape(slots, width)

    def add(src, b):
        chosen = hits_t[:, lanes_of(src, b)]
        ctf = ctf_got[src, frames_of(b)]
        square = (ctf * ctf)[None] * spec_got[src, b, :, :, :1].astype(F32)
        parts = jnp.concatenate(split(square.reshape(slots, cycles)), axis=1)
        norms[...] += jnp.dot(chosen, parts, preferred_element_type=F32)
        for i in range(sums.shape[0]):
            sums[i] += jnp.dot(
                chosen, slot_terms(src, b, other_half + i), preferred_element_type=F32
            )

    for b in range(BATCHES):
        add(chip, b)
    for b in range(BATCHES):

        @pl.loop(1, chips)
        def _(off):
            spec_copy(off, b).wait_recv()
            add(chip_at(-off), b)

    for b in range(BATCHES):
        for off in range(1, chips):
            part_copy(off, b).wait_send()
            score_copy(off, b).wait_send()
            spec_copy(off, b).wait_send()
    norms[:, :cycles] += norms[:, cycles:]

    if not deliver:
        sum_out[...] = sums[...].astype(BF16)
        norm_out[...] = norms[:, :cycles]
        return

    mine = pl.multiple_of(me * owned, owned)
    other = pl.multiple_of(sibling[1] * owned, owned)
    half_send[...] = sums[...].astype(BF16)
    half_norm[...] = norms[pl.ds(other, owned), :]
    sum_half = remote(half_send, half_got, half_sem, (0,), sibling)
    norm_half = remote(half_norm, half_norm_got, half_sem, (1,), sibling)
    sum_half.start()
    norm_half.start()
    def sum_copy(a, b):
        to = peer(a, b)
        start = pl.multiple_of(to[1] * owned, owned)
        src = sum_send.at[pl.ds(to[0] * run, run), pl.ds(start, owned), :]
        return remote(src, sum_got.at[dom, me], sum_sem, (a, b), to)

    def norm_copy(a):
        return remote(norm_send, norm_got.at[dom], norm_sem, (a,), peer(a, 0))

    waited = False
    for a in sorted(range(doms), key=lambda a: (a == 0, abs(a - doms // 2))):
        first = peer(a, 0)[0] * run
        own = []
        for one in range(run):
            for src in range(chips):
                for b in range(BATCHES):
                    at = pl.ds((src * BATCHES + b) * slots, slots)
                    terms[one, at, :] = slot_terms(src, b, own_half + first + one)
            own.append(jnp.dot(hits_t[...], terms[one], preferred_element_type=F32))
        if not waited:
            sum_half.wait()
            norm_half.wait()
            norm_send[...] = norms[pl.ds(mine, owned), :] + half_norm_got[...]
            waited = True
        for one in range(run):
            both = own[one] + half_got[first + one].astype(F32)
            sum_send[first + one] = both.astype(BF16)
        for b in range(owners):
            if (a, b) in offsets:
                sum_copy(a, b).start()
        if a:
            norm_copy(a).start()
    sum_got[dom, me] = sum_send[pl.ds(dom * run, run), pl.ds(mine, owned), :]
    norm_got[dom] = norm_send[...]
    for a, b in offsets:
        sum_copy(a, b).wait()
    for a in range(1, doms):
        norm_copy(a).wait()


def finish_body(cycles, sum_ref, norm_ref, out_ref, low, high):
    doms, owners, run, owned, width = sum_ref.shape
    harm = width // 2
    held = owners * run
    dom = lax.axis_index("dom")
    norms = norm_ref[0, :, :cycles]
    for a in range(1, doms):
        norms = norms + norm_ref[a, :, :cycles]
    for c in range(owners):
        for one in range(run):
            cycle = c * run + one
            result = sum_ref[0, c, one].astype(F32)
            for a in range(1, doms):
                result = result + sum_ref[a, c, one].astype(F32)
            result = result / (column(norms, dom * held + cycle) + 1.0)
            at = pl.ds(cycle, owned, stride=held)
            low[at, :] = result[:, :harm]
            high[at, :] = result[:, harm:]
    out_ref[:, :harm] = low[...]
    out_ref[:, harm:] = high[...]


def on_device(doms, images, references, ctf_table, defocus, priors):
    owners = lax.axis_size("cls")
    particles, cycles, angles = images.shape
    owned = references.shape[0]
    classes = owners * owned
    prior_count = priors.shape[1]
    chips = owners // CORES
    share = cycles // chips
    width = angles // 2 * 2
    held = cycles // doms
    deliver = held % owners == 0
    run = max(held // owners, 1)
    forward, inverse = (jnp.asarray(t) for t in angle_tables(angles))
    swap = jnp.asarray(swap_matrix(), BF16)
    if deliver:
        shapes = [
            jax.ShapeDtypeStruct((doms, owners, run, owned, width), BF16),
            jax.ShapeDtypeStruct((doms, owned, 2 * cycles), F32),
        ]
    else:
        shapes = [
            jax.ShapeDtypeStruct((share, classes, width), BF16),
            jax.ShapeDtypeStruct((classes, cycles), F32),
        ]
    batch = particles // BATCHES
    slots = (BATCHES, prior_count, batch, width)
    rows = prior_count * batch
    sums = (share, classes, width)
    half = (doms * run, classes, width)
    pair_sem = pltpu.SemaphoreType.DMA((2, chips))
    batch_sem = pltpu.SemaphoreType.DMA((2, chips, BATCHES))
    done = pl.pallas_call(
        functools.partial(body, doms, chips, prior_count, deliver),
        out_shape=shapes,
        in_specs=[pl.BlockSpec(memory_space=pl.ANY)] + [VMEM] * 7,
        out_specs=[VMEM] * len(shapes),
        scratch_shapes=[
            pltpu.VMEM(images.shape, BF16),
            pltpu.VMEM((chips, share, particles, width), BF16),
            pltpu.VMEM((chips, share, particles, width), BF16),
            pltpu.VMEM((chips, share, owned, width), BF16),
            pltpu.VMEM((owners, share, owned, width), BF16),
            pltpu.VMEM((16, 128), jnp.int32),
            pltpu.VMEM((chips, 16, 128), jnp.int32),
            pltpu.VMEM((chips, share, particles, width), BF16),
            pltpu.VMEM((chips, particles, cycles), F32),
            pltpu.VMEM((chips, BATCHES, rows, classes), BF16),
            pltpu.VMEM((classes, chips * BATCHES * rows), BF16),
            pltpu.VMEM((run, chips * BATCHES * rows, width), BF16),
            pltpu.VMEM((chips,) + slots, BF16),
            pltpu.VMEM((chips,) + slots, BF16),
            pltpu.VMEM(slots, BF16),
            pltpu.VMEM((chips,) + slots, BF16),
            pltpu.VMEM(half if deliver else sums, F32),
            pltpu.VMEM((classes, 2 * cycles), F32),
            pltpu.VMEM(half, BF16),
            pltpu.VMEM(half, BF16),
            pltpu.VMEM((owned, 2 * cycles), F32),
            pltpu.VMEM((owned, 2 * cycles), F32),
            pltpu.VMEM(half, BF16),
            pltpu.VMEM((owned, 2 * cycles), F32),
            pltpu.SemaphoreType.DMA,
            pair_sem,
            pair_sem,
            pair_sem,
            batch_sem,
            batch_sem,
            batch_sem,
            pltpu.SemaphoreType.DMA((2, 2)),
            pltpu.SemaphoreType.DMA((2, doms, owners)),
            pltpu.SemaphoreType.DMA((2, doms)),
        ],
        compiler_params=pltpu.CompilerParams(
            collective_id=1, has_side_effects=True, vmem_limit_bytes=LIMIT
        ),
    )(images, references, priors.T, defocus[None, :], ctf_table, swap, forward, inverse)
    if deliver:
        done = pl.pallas_call(
            functools.partial(finish_body, cycles),
            out_shape=jax.ShapeDtypeStruct((owned * held, width), F32),
            in_specs=[VMEM] * 2,
            out_specs=VMEM,
            scratch_shapes=[pltpu.VMEM((owned * held, width // 2), F32)] * 2,
            compiler_params=pltpu.CompilerParams(vmem_limit_bytes=LIMIT),
        )(*done)
        return done.reshape(owned, held, width)
    sums, norms = done
    me = lax.axis_index("cls")
    chip = me // CORES
    mine = chip * share + jnp.arange(share)
    placed = jnp.zeros((cycles, classes, width), F32).at[mine].set(sums.astype(F32))
    placed = lax.psum_scatter(placed, "dom", scatter_dimension=0, tiled=True)
    placed = lax.psum_scatter(placed, "cls", scatter_dimension=1, tiled=True)
    rows = jnp.arange(classes)[:, None] // (CORES * owned)
    norms = jnp.where(rows == chip, norms, 0.0)
    norms = lax.psum_scatter(norms, "dom", scatter_dimension=1, tiled=True)
    norms = lax.psum_scatter(norms, "cls", scatter_dimension=0, tiled=True)
    return placed.transpose(1, 0, 2) / (norms + 1.0)[:, :, None]


def solution(mesh):
    return jax.shard_map(
        functools.partial(on_device, mesh.shape["dom"]),
        mesh=mesh,
        in_specs=(
            P(("dom", "cls"), None, None),
            P("cls", None, None),
            P(),
            P(("dom", "cls")),
            P(("dom", "cls"), None),
        ),
        out_specs=P("cls", "dom", None),
        check_vma=False,
    )
```

```python
import functools

import jax
import jax.numpy as jnp
import numpy as np
from jax import lax
from jax.experimental import pallas as pl
from jax.experimental.pallas import tpu as pltpu
from jax.sharding import PartitionSpec as P

MESH = pl.DeviceIdType.MESH
VMEM = pl.BlockSpec(memory_space=pltpu.VMEM)
LIMIT = 56 * 1024 * 1024
F32 = jnp.float32
BF16 = jnp.bfloat16
EXACT = lax.Precision.HIGHEST
TILE = 16
CORES = 2
BATCHES = 2


def angle_tables(angles):
    harm_count = angles // 2
    phase = np.arange(angles)[:, None] * np.arange(harm_count)[None, :] % angles
    grid = 2.0 * np.pi / angles * phase
    cosine, sine = np.cos(grid), np.sin(grid)
    forward = np.concatenate([cosine, sine], axis=1)
    weight = np.where(np.arange(harm_count) == 0, 1.0, 2.0)[:, None] / angles
    inverse = np.concatenate([cosine.T * weight, -sine.T * weight], axis=0)
    return forward.astype(np.float32), inverse.astype(np.float32)


def swap_matrix():
    rows = np.arange(TILE * TILE)
    swap = np.zeros((TILE * TILE, TILE * TILE), np.float32)
    swap[rows, rows % TILE * TILE + rows // TILE] = 1.0
    return swap


def harmonics(src, dst, swap, table, place, frames):
    cycles, angles = src.shape[1:]
    for first in range(0, cycles, TILE):
        for frame in range(*frames, TILE):
            block = src[frame : frame + TILE, first : first + TILE, :]
            block = block.reshape(TILE * TILE, angles)
            block = jnp.dot(swap, block, preferred_element_type=F32).astype(BF16)
            out = jnp.dot(block, table, preferred_element_type=F32).astype(BF16)
            for r in range(TILE):
                chip, s = place(first + r)
                dst[chip, s, frame : frame + TILE, :] = out[r * TILE : (r + 1) * TILE]


def column(rows, index):
    lanes = lax.broadcasted_iota(jnp.int32, rows.shape, 1)
    return jnp.sum(jnp.where(lanes == index, rows, 0.0), axis=1, keepdims=True)


def class_hits(meta, priors, classes):
    lanes = lax.broadcasted_iota(jnp.int32, (meta.shape[0], classes), 1)
    return jnp.concatenate(
        [(meta[:, j : j + 1] == lanes).astype(F32) for j in range(priors)], axis=0
    )


def split(rows):
    high = rows.astype(BF16)
    return high, (rows - high.astype(F32)).astype(BF16)


def table_product(rows, table):
    high, low = split(rows)
    table_high, table_low = split(table)
    total = jnp.dot(high, table_low, preferred_element_type=F32)
    total = total + jnp.dot(low, table_high, preferred_element_type=F32)
    return total + jnp.dot(high, table_high, preferred_element_type=F32)


def ctf_rows(meta, priors, table):
    groups = table.shape[0]
    lanes = lax.broadcasted_iota(jnp.int32, (meta.shape[0], groups), 1)
    hits = (meta[:, priors : priors + 1] == lanes).astype(F32)
    return jnp.dot(hits, table, precision=EXACT, preferred_element_type=F32)


def body(
    doms,
    chips,
    priors,
    deliver,
    img_ref,
    ref_ref,
    priors_ref,
    defocus_ref,
    ctf_ref,
    swap_ref,
    forward_ref,
    inverse_ref,
    *rest,
):
    if deliver:
        sum_got, norm_got, rest = rest[0], rest[1], rest[2:]
    else:
        sum_out, norm_out, rest = rest[0], rest[1], rest[2:]
    (
        img_got,
        part_send,
        part_got,
        cls_send,
        cls_got,
        meta_send,
        meta_got,
        scaled,
        ctf_got,
        hits,
        hits_t,
        terms,
        score_send,
        score_got,
        spec_send,
        spec_got,
        sums,
        norms,
        half_send,
        half_got,
        half_norm,
        half_norm_got,
        sum_send,
        norm_send,
        img_sem,
        cls_sem,
        cross_sem,
        pass_sem,
        meta_sem,
        part_sem,
        score_sem,
        spec_sem,
        half_sem,
        sum_sem,
        norm_sem,
    ) = rest
    dom, me = lax.axis_index("dom"), lax.axis_index("cls")
    chip, core = me // CORES, me % CORES
    sibling = (dom, me + 1 - 2 * core)
    particles, cycles, angles = img_ref.shape
    batch = particles // BATCHES
    slots = priors * batch
    owned = ref_ref.shape[0]
    owners = chips * CORES
    classes = owners * owned
    share = cycles // chips
    harm = angles // 2
    width = 2 * harm
    held = cycles // doms
    run = max(held // owners, 1)

    def place(r):
        if not deliver:
            return r // share, r % share
        to, chip, half, one = r // held, r % held // (CORES * run), r // run % CORES, r % run
        return chip, (half * doms + to) * run + one

    places = {place(r): r for r in range(cycles)}
    first_cycle = [places[0, s] for s in range(share)]
    chip_step = places[1, 0] - places[0, 0]

    barrier = pltpu.get_barrier_semaphore()
    offsets = [(a, b) for a in range(doms) for b in range(owners)][1:]

    def peer(a, b):
        return (lax.rem(dom + a, doms), lax.rem(me + b, owners))

    def chip_at(off):
        number, bit = 0, 1
        while bit < chips:
            ours, flip = chip // bit % 2, off // bit % 2
            number = number + bit * (ours + flip - 2 * ours * flip)
            bit *= 2
        return number

    def remote(src, dst, sem, at, device):
        return pltpu.make_async_remote_copy(
            src_ref=src,
            dst_ref=dst,
            send_sem=sem.at[(0,) + at],
            recv_sem=sem.at[(1,) + at],
            device_id=device,
            device_id_type=MESH,
        )

    def same_core(off):
        return (dom, chip_at(off) * CORES + core)

    upper = dom % 2
    partner = (dom + 1 - 2 * upper, me)
    part_share = share // 2

    def cycle_half(h):
        return pl.ds((upper + h - 2 * upper * h) * part_share, part_share)

    def cls_copy(off):
        src = cls_send.at[chip_at(off), cycle_half(0)]
        return remote(src, cls_got.at[me, cycle_half(0)], cls_sem, (off,), same_core(off))

    def cross_copy(off):
        slot = cls_got.at[chip_at(off) * CORES + core, cycle_half(0)]
        return remote(slot, slot, cross_sem, (off,), partner)

    def cross_got(off):
        slot = cls_got.at[chip_at(off) * CORES + core, cycle_half(1)]
        return remote(slot, slot, cross_sem, (off,), partner)

    def pass_copy(off, h):
        slot = cls_got.at[chip_at(off) * CORES + core, cycle_half(h)]
        return remote(slot, slot, pass_sem, (off, h), sibling)

    def pass_got(off, h):
        slot = cls_got.at[chip_at(off) * CORES + 1 - core, cycle_half(h)]
        return remote(slot, slot, pass_sem, (off, h), sibling)

    def meta_copy(off):
        return remote(meta_send, meta_got.at[chip], meta_sem, (off,), same_core(off))

    def frames_of(b):
        return pl.ds(b * batch, batch)

    def part_copy(off, b):
        return remote(
            part_send.at[chip_at(off), :, frames_of(b), :],
            part_got.at[chip, :, frames_of(b), :],
            part_sem,
            (off, b),
            same_core(off),
        )

    def score_copy(off, b):
        return remote(
            score_send.at[chip_at(off), b],
            score_got.at[chip, b],
            score_sem,
            (off, b),
            same_core(off),
        )

    def spec_copy(off, b):
        return remote(spec_send.at[b], spec_got.at[chip, b], spec_sem, (off, b), same_core(off))

    images = pltpu.make_async_copy(img_ref, img_got, img_sem)
    images.start()
    for a, b in offsets:
        pl.semaphore_signal(barrier, inc=1, device_id=peer(a, b), device_id_type=MESH)
    meta_send[...] = jnp.zeros_like(meta_send)
    meta_send[:priors, :particles] = priors_ref[...]
    meta_send[priors : priors + 1, :particles] = defocus_ref[...]
    table = forward_ref[...].astype(BF16)
    swap = swap_ref[...]
    harmonics(ref_ref, cls_send, swap, table, place, (0, owned))
    cls_got[me] = cls_send[chip]
    pl.semaphore_wait(barrier, len(offsets))
    for off in range(1, chips):
        meta_copy(off).start()
        cls_copy(off).start()
    for h in range(2):
        pass_copy(0, h).start()
    images.wait()
    for b in range(BATCHES):
        harmonics(img_got, part_send, swap, table, place, (b * batch, (b + 1) * batch))
        for off in range(1, chips):
            part_copy(off, b).start()
    part_got[chip] = part_send[chip]
    meta_got[chip] = meta_send[...]
    sums[...] = jnp.zeros_like(sums)
    norms[...] = jnp.zeros_like(norms)
    for off in range(1, chips):
        cls_copy(off).wait_recv()
        cross_copy(off).start()
        pass_copy(off, 0).start()
    for off in range(1, chips):
        meta_copy(off).wait()

    def lanes_of(src, b):
        return pl.ds(pl.multiple_of((src * BATCHES + b) * slots, slots), slots)

    @pl.loop(0, chips)
    def _(src):
        meta = meta_got[src].astype(F32).T[:particles].astype(jnp.int32)
        ctf_got[src] = ctf_rows(meta, priors, ctf_ref[...])
        for b in range(BATCHES):
            found = class_hits(meta[b * batch : (b + 1) * batch], priors, classes)
            hits[src, b] = found.astype(BF16)
            hits_t[:, lanes_of(src, b)] = found.T.astype(BF16)

    for off in range(1, chips):
        cross_got(off).wait_recv()
        pass_copy(off, 1).start()
    for off in range(1, chips):
        cls_copy(off).wait_send()
        cross_copy(off).wait_send()
    for off in range(chips):
        for h in range(2):
            pass_copy(off, h).wait_send()
            pass_got(off, h).wait_recv()

    def score(src, b):
        ctf = ctf_got[src, frames_of(b)]
        real, imag = 0.0, 0.0
        for s in range(share):
            part = part_got[src, s, frames_of(b)].astype(F32)
            part = part * column(ctf, first_cycle[s] + chip_step * chip)
            scaled[src, s, frames_of(b)] = part.astype(BF16)
            table = cls_got[:, s].reshape(classes, width)
            picked = jnp.dot(hits[src, b], table, preferred_element_type=F32)
            picked = picked.reshape(priors, batch, width)
            pc, ps = part[None, :, :harm], part[None, :, harm:]
            cc, cs = picked[:, :, :harm], picked[:, :, harm:]
            real = real + (pc * cc + ps * cs)
            imag = imag + (pc * cs - ps * cc)
        score_send[src, b, :, :, :harm] = real.astype(BF16)
        score_send[src, b, :, :, harm:] = imag.astype(BF16)

    for b in range(BATCHES):
        score(chip, b)
    for b in range(BATCHES):

        @pl.loop(1, chips)
        def _(off):
            part_copy(off, b).wait_recv()
            score(chip_at(off), b)
            score_copy(off, b).start()

    for b in range(BATCHES):
        joined = score_send[chip, b].astype(F32)
        for off in range(1, chips):
            score_copy(off, b).wait_recv()
            joined = joined + score_got[chip_at(off), b].astype(F32)
        scores = table_product(joined.reshape(slots, width), inverse_ref[...])
        scores = scores.reshape(priors, batch, angles)
        highest = jnp.max(jnp.max(scores, axis=0), axis=1, keepdims=True)
        total = jnp.sum(jnp.exp(scores - highest[None]), axis=0)
        log_total = highest + jnp.log(jnp.sum(total, axis=1, keepdims=True))
        weights = jnp.exp(scores - log_total[None]).reshape(slots, angles)
        spectrum = table_product(weights, forward_ref[...])
        spec_send[b] = spectrum.astype(BF16).reshape(priors, batch, width)
        for off in range(1, chips):
            spec_copy(off, b).start()
        spec_got[chip, b] = spec_send[b]

    half = doms * run
    other_half, own_half = ((1 - core) * half, core * half) if deliver else (0, 0)

    def slot_terms(src, b, s):
        spectrum = spec_got[src, b]
        wc, ws = spectrum[:, :, :harm], spectrum[:, :, harm:]
        part = scaled[src, s, frames_of(b)][None]
        pc, ps = part[:, :, :harm], part[:, :, harm:]
        both = jnp.concatenate([pc * wc + ps * ws, ps * wc - pc * ws], axis=2)
        return both.reshape(slots, width)

    def add(src, b):
        chosen = hits_t[:, lanes_of(src, b)]
        ctf = ctf_got[src, frames_of(b)]
        square = (ctf * ctf)[None] * spec_got[src, b, :, :, :1].astype(F32)
        parts = jnp.concatenate(split(square.reshape(slots, cycles)), axis=1)
        norms[...] += jnp.dot(chosen, parts, preferred_element_type=F32)
        for i in range(sums.shape[0]):
            sums[i] += jnp.dot(
                chosen, slot_terms(src, b, other_half + i), preferred_element_type=F32
            )

    for b in range(BATCHES):
        add(chip, b)
    for b in range(BATCHES):

        @pl.loop(1, chips)
        def _(off):
            spec_copy(off, b).wait_recv()
            add(chip_at(off), b)

    for b in range(BATCHES):
        for off in range(1, chips):
            part_copy(off, b).wait_send()
            score_copy(off, b).wait_send()
            spec_copy(off, b).wait_send()
    norms[:, :cycles] += norms[:, cycles:]

    if not deliver:
        sum_out[...] = sums[...].astype(BF16)
        norm_out[...] = norms[:, :cycles]
        return

    mine = pl.multiple_of(me * owned, owned)
    other = pl.multiple_of(sibling[1] * owned, owned)
    half_send[...] = sums[...].astype(BF16)
    half_norm[...] = norms[pl.ds(other, owned), :]
    sum_half = remote(half_send, half_got, half_sem, (0,), sibling)
    norm_half = remote(half_norm, half_norm_got, half_sem, (1,), sibling)
    sum_half.start()
    norm_half.start()
    def sum_copy(a, b):
        to = peer(a, b)
        start = pl.multiple_of(to[1] * owned, owned)
        src = sum_send.at[pl.ds(to[0] * run, run), pl.ds(start, owned), :]
        return remote(src, sum_got.at[dom, me], sum_sem, (a, b), to)

    def norm_copy(a):
        return remote(norm_send, norm_got.at[dom], norm_sem, (a,), peer(a, 0))

    waited = False
    for a in sorted(range(doms), key=lambda a: (a == 0, abs(a - doms // 2))):
        first = peer(a, 0)[0] * run
        own = []
        for one in range(run):
            for src in range(chips):
                for b in range(BATCHES):
                    at = pl.ds((src * BATCHES + b) * slots, slots)
                    terms[one, at, :] = slot_terms(src, b, own_half + first + one)
            own.append(jnp.dot(hits_t[...], terms[one], preferred_element_type=F32))
        if not waited:
            sum_half.wait()
            norm_half.wait()
            norm_send[...] = norms[pl.ds(mine, owned), :] + half_norm_got[...]
            waited = True
        for one in range(run):
            both = own[one] + half_got[first + one].astype(F32)
            sum_send[first + one] = both.astype(BF16)
        for b in range(owners):
            if (a, b) in offsets:
                sum_copy(a, b).start()
        if a:
            norm_copy(a).start()
    sum_got[dom, me] = sum_send[pl.ds(dom * run, run), pl.ds(mine, owned), :]
    norm_got[dom] = norm_send[...]
    for a, b in offsets:
        sum_copy(a, b).wait()
    for a in range(1, doms):
        norm_copy(a).wait()


def finish_body(cycles, sum_ref, norm_ref, out_ref, low, high):
    doms, owners, run, owned, width = sum_ref.shape
    harm = width // 2
    held = owners * run
    dom = lax.axis_index("dom")
    norms = norm_ref[0, :, :cycles]
    for a in range(1, doms):
        norms = norms + norm_ref[a, :, :cycles]
    for c in range(owners):
        for one in range(run):
            cycle = c * run + one
            result = sum_ref[0, c, one].astype(F32)
            for a in range(1, doms):
                result = result + sum_ref[a, c, one].astype(F32)
            result = result / (column(norms, dom * held + cycle) + 1.0)
            at = pl.ds(cycle, owned, stride=held)
            low[at, :] = result[:, :harm]
            high[at, :] = result[:, harm:]
    out_ref[:, :harm] = low[...]
    out_ref[:, harm:] = high[...]


def on_device(doms, images, references, ctf_table, defocus, priors):
    owners = lax.axis_size("cls")
    particles, cycles, angles = images.shape
    owned = references.shape[0]
    classes = owners * owned
    prior_count = priors.shape[1]
    chips = owners // CORES
    share = cycles // chips
    width = angles // 2 * 2
    held = cycles // doms
    deliver = held % owners == 0
    run = max(held // owners, 1)
    forward, inverse = (jnp.asarray(t) for t in angle_tables(angles))
    swap = jnp.asarray(swap_matrix(), BF16)
    if deliver:
        shapes = [
            jax.ShapeDtypeStruct((doms, owners, run, owned, width), BF16),
            jax.ShapeDtypeStruct((doms, owned, 2 * cycles), F32),
        ]
    else:
        shapes = [
            jax.ShapeDtypeStruct((share, classes, width), BF16),
            jax.ShapeDtypeStruct((classes, cycles), F32),
        ]
    batch = particles // BATCHES
    slots = (BATCHES, prior_count, batch, width)
    rows = prior_count * batch
    sums = (share, classes, width)
    half = (doms * run, classes, width)
    pair_sem = pltpu.SemaphoreType.DMA((2, chips))
    batch_sem = pltpu.SemaphoreType.DMA((2, chips, BATCHES))
    done = pl.pallas_call(
        functools.partial(body, doms, chips, prior_count, deliver),
        out_shape=shapes,
        in_specs=[pl.BlockSpec(memory_space=pl.ANY)] + [VMEM] * 7,
        out_specs=[VMEM] * len(shapes),
        scratch_shapes=[
            pltpu.VMEM(images.shape, BF16),
            pltpu.VMEM((chips, share, particles, width), BF16),
            pltpu.VMEM((chips, share, particles, width), BF16),
            pltpu.VMEM((chips, share, owned, width), BF16),
            pltpu.VMEM((owners, share, owned, width), BF16),
            pltpu.VMEM((16, 128), jnp.int32),
            pltpu.VMEM((chips, 16, 128), jnp.int32),
            pltpu.VMEM((chips, share, particles, width), BF16),
            pltpu.VMEM((chips, particles, cycles), F32),
            pltpu.VMEM((chips, BATCHES, rows, classes), BF16),
            pltpu.VMEM((classes, chips * BATCHES * rows), BF16),
            pltpu.VMEM((run, chips * BATCHES * rows, width), BF16),
            pltpu.VMEM((chips,) + slots, BF16),
            pltpu.VMEM((chips,) + slots, BF16),
            pltpu.VMEM(slots, BF16),
            pltpu.VMEM((chips,) + slots, BF16),
            pltpu.VMEM(half if deliver else sums, F32),
            pltpu.VMEM((classes, 2 * cycles), F32),
            pltpu.VMEM(half, BF16),
            pltpu.VMEM(half, BF16),
            pltpu.VMEM((owned, 2 * cycles), F32),
            pltpu.VMEM((owned, 2 * cycles), F32),
            pltpu.VMEM(half, BF16),
            pltpu.VMEM((owned, 2 * cycles), F32),
            pltpu.SemaphoreType.DMA,
            pair_sem,
            pair_sem,
            pltpu.SemaphoreType.DMA((2, chips, 2)),
            pair_sem,
            batch_sem,
            batch_sem,
            batch_sem,
            pltpu.SemaphoreType.DMA((2, 2)),
            pltpu.SemaphoreType.DMA((2, doms, owners)),
            pltpu.SemaphoreType.DMA((2, doms)),
        ],
        compiler_params=pltpu.CompilerParams(
            collective_id=1, has_side_effects=True, vmem_limit_bytes=LIMIT
        ),
    )(images, references, priors.T, defocus[None, :], ctf_table, swap, forward, inverse)
    if deliver:
        done = pl.pallas_call(
            functools.partial(finish_body, cycles),
            out_shape=jax.ShapeDtypeStruct((owned * held, width), F32),
            in_specs=[VMEM] * 2,
            out_specs=VMEM,
            scratch_shapes=[pltpu.VMEM((owned * held, width // 2), F32)] * 2,
            compiler_params=pltpu.CompilerParams(vmem_limit_bytes=LIMIT),
        )(*done)
        return done.reshape(owned, held, width)
    sums, norms = done
    me = lax.axis_index("cls")
    chip = me // CORES
    mine = chip * share + jnp.arange(share)
    placed = jnp.zeros((cycles, classes, width), F32).at[mine].set(sums.astype(F32))
    placed = lax.psum_scatter(placed, "dom", scatter_dimension=0, tiled=True)
    placed = lax.psum_scatter(placed, "cls", scatter_dimension=1, tiled=True)
    rows = jnp.arange(classes)[:, None] // (CORES * owned)
    norms = jnp.where(rows == chip, norms, 0.0)
    norms = lax.psum_scatter(norms, "dom", scatter_dimension=1, tiled=True)
    norms = lax.psum_scatter(norms, "cls", scatter_dimension=0, tiled=True)
    return placed.transpose(1, 0, 2) / (norms + 1.0)[:, :, None]


def solution(mesh):
    return jax.shard_map(
        functools.partial(on_device, mesh.shape["dom"]),
        mesh=mesh,
        in_specs=(
            P(("dom", "cls"), None, None),
            P("cls", None, None),
            P(),
            P(("dom", "cls")),
            P(("dom", "cls"), None),
        ),
        out_specs=P("cls", "dom", None),
        check_vma=False,
    )
```

```python
import functools

import jax
import jax.numpy as jnp
import numpy as np
from jax import lax
from jax.experimental import pallas as pl
from jax.experimental.pallas import tpu as pltpu
from jax.sharding import PartitionSpec as P

MESH = pl.DeviceIdType.MESH
VMEM = pl.BlockSpec(memory_space=pltpu.VMEM)
LIMIT = 56 * 1024 * 1024
F32 = jnp.float32
BF16 = jnp.bfloat16
EXACT = lax.Precision.HIGHEST
TILE = 16
CORES = 2
BATCHES = 2


def angle_tables(angles):
    harm_count = angles // 2
    phase = np.arange(angles)[:, None] * np.arange(harm_count)[None, :] % angles
    grid = 2.0 * np.pi / angles * phase
    cosine, sine = np.cos(grid), np.sin(grid)
    forward = np.concatenate([cosine, sine], axis=1)
    weight = np.where(np.arange(harm_count) == 0, 1.0, 2.0)[:, None] / angles
    inverse = np.concatenate([cosine.T * weight, -sine.T * weight], axis=0)
    return forward.astype(np.float32), inverse.astype(np.float32)


def swap_matrix():
    rows = np.arange(TILE * TILE)
    swap = np.zeros((TILE * TILE, TILE * TILE), np.float32)
    swap[rows, rows % TILE * TILE + rows // TILE] = 1.0
    return swap


def harmonics(src, dst, swap, table, place, frames):
    cycles, angles = src.shape[1:]
    for first in range(0, cycles, TILE):
        for frame in range(*frames, TILE):
            block = src[frame : frame + TILE, first : first + TILE, :]
            block = block.reshape(TILE * TILE, angles)
            block = jnp.dot(swap, block, preferred_element_type=F32).astype(BF16)
            out = jnp.dot(block, table, preferred_element_type=F32).astype(BF16)
            for r in range(TILE):
                chip, s = place(first + r)
                dst[chip, s, frame : frame + TILE, :] = out[r * TILE : (r + 1) * TILE]


def column(rows, index):
    lanes = lax.broadcasted_iota(jnp.int32, rows.shape, 1)
    return jnp.sum(jnp.where(lanes == index, rows, 0.0), axis=1, keepdims=True)


def class_hits(meta, priors, classes):
    lanes = lax.broadcasted_iota(jnp.int32, (meta.shape[0], classes), 1)
    return jnp.concatenate(
        [(meta[:, j : j + 1] == lanes).astype(F32) for j in range(priors)], axis=0
    )


def split(rows):
    high = rows.astype(BF16)
    return high, (rows - high.astype(F32)).astype(BF16)


def table_product(rows, table):
    high, low = split(rows)
    table_high, table_low = split(table)
    total = jnp.dot(high, table_low, preferred_element_type=F32)
    total = total + jnp.dot(low, table_high, preferred_element_type=F32)
    return total + jnp.dot(high, table_high, preferred_element_type=F32)


def ctf_rows(meta, priors, table):
    groups = table.shape[0]
    lanes = lax.broadcasted_iota(jnp.int32, (meta.shape[0], groups), 1)
    hits = (meta[:, priors : priors + 1] == lanes).astype(F32)
    return jnp.dot(hits, table, precision=EXACT, preferred_element_type=F32)


def body(
    doms,
    chips,
    priors,
    deliver,
    img_ref,
    ref_ref,
    priors_ref,
    defocus_ref,
    ctf_ref,
    swap_ref,
    forward_ref,
    inverse_ref,
    *rest,
):
    if deliver:
        sum_got, norm_got, rest = rest[0], rest[1], rest[2:]
    else:
        sum_out, norm_out, rest = rest[0], rest[1], rest[2:]
    (
        img_got,
        part_send,
        part_got,
        cls_send,
        cls_got,
        meta_send,
        meta_got,
        scaled,
        ctf_got,
        hits,
        hits_t,
        terms,
        score_send,
        score_got,
        spec_send,
        spec_got,
        sums,
        norms,
        half_send,
        half_got,
        half_norm,
        half_norm_got,
        sum_send,
        norm_send,
        img_sem,
        cls_sem,
        cross_sem,
        pass_sem,
        meta_sem,
        part_sem,
        score_sem,
        spec_sem,
        half_sem,
        sum_sem,
        norm_sem,
    ) = rest
    dom, me = lax.axis_index("dom"), lax.axis_index("cls")
    chip, core = me // CORES, me % CORES
    sibling = (dom, me + 1 - 2 * core)
    particles, cycles, angles = img_ref.shape
    batch = particles // BATCHES
    slots = priors * batch
    owned = ref_ref.shape[0]
    owners = chips * CORES
    classes = owners * owned
    share = cycles // chips
    harm = angles // 2
    width = 2 * harm
    held = cycles // doms
    run = max(held // owners, 1)

    def place(r):
        if not deliver:
            return r // share, r % share
        to, chip, half, one = r // held, r % held // (CORES * run), r // run % CORES, r % run
        return chip, (half * doms + to) * run + one

    places = {place(r): r for r in range(cycles)}
    first_cycle = [places[0, s] for s in range(share)]
    chip_step = places[1, 0] - places[0, 0]

    barrier = pltpu.get_barrier_semaphore()
    offsets = [(a, b) for a in range(doms) for b in range(owners)][1:]

    def peer(a, b):
        return (lax.rem(dom + a, doms), lax.rem(me + b, owners))

    def chip_at(off):
        number, bit = 0, 1
        while bit < chips:
            ours, flip = chip // bit % 2, off // bit % 2
            number = number + bit * (ours + flip - 2 * ours * flip)
            bit *= 2
        return number

    def remote(src, dst, sem, at, device):
        return pltpu.make_async_remote_copy(
            src_ref=src,
            dst_ref=dst,
            send_sem=sem.at[(0,) + at],
            recv_sem=sem.at[(1,) + at],
            device_id=device,
            device_id_type=MESH,
        )

    def same_core(off):
        return (dom, chip_at(off) * CORES + core)

    upper = dom % 2
    partner = (dom + 1 - 2 * upper, me)
    part_share = share // 2

    def cycle_half(h):
        return pl.ds((upper + h - 2 * upper * h) * part_share, part_share)

    def cls_copy(off):
        src = cls_send.at[chip_at(off), cycle_half(0)]
        return remote(src, cls_got.at[me, cycle_half(0)], cls_sem, (off,), same_core(off))

    def cross_copy(off):
        slot = cls_got.at[chip_at(off) * CORES + core, cycle_half(0)]
        return remote(slot, slot, cross_sem, (off,), partner)

    def cross_got(off):
        slot = cls_got.at[chip_at(off) * CORES + core, cycle_half(1)]
        return remote(slot, slot, cross_sem, (off,), partner)

    def pass_copy(off, h):
        slot = cls_got.at[chip_at(off) * CORES + core, cycle_half(h)]
        return remote(slot, slot, pass_sem, (off, h), sibling)

    def pass_got(off, h):
        slot = cls_got.at[chip_at(off) * CORES + 1 - core, cycle_half(h)]
        return remote(slot, slot, pass_sem, (off, h), sibling)

    def meta_copy(off):
        return remote(meta_send, meta_got.at[chip], meta_sem, (off,), same_core(off))

    def frames_of(b):
        return pl.ds(b * batch, batch)

    def part_copy(off, b):
        return remote(
            part_send.at[chip_at(off), :, frames_of(b), :],
            part_got.at[chip, :, frames_of(b), :],
            part_sem,
            (off, b),
            same_core(off),
        )

    def score_copy(off, b):
        return remote(
            score_send.at[chip_at(off), b],
            score_got.at[chip, b],
            score_sem,
            (off, b),
            same_core(off),
        )

    def spec_copy(off, b):
        return remote(spec_send.at[b], spec_got.at[chip, b], spec_sem, (off, b), same_core(off))

    images = pltpu.make_async_copy(img_ref, img_got, img_sem)
    images.start()
    for a, b in offsets:
        pl.semaphore_signal(barrier, inc=1, device_id=peer(a, b), device_id_type=MESH)
    meta_send[...] = jnp.zeros_like(meta_send)
    meta_send[:priors, :particles] = priors_ref[...]
    meta_send[priors : priors + 1, :particles] = defocus_ref[...]
    table = forward_ref[...].astype(BF16)
    swap = swap_ref[...]
    harmonics(ref_ref, cls_send, swap, table, place, (0, owned))
    cls_got[me] = cls_send[chip]
    pl.semaphore_wait(barrier, len(offsets))
    for off in range(1, chips):
        meta_copy(off).start()
        cls_copy(off).start()
    for h in range(2):
        pass_copy(0, h).start()
    images.wait()
    for b in range(BATCHES):
        harmonics(img_got, part_send, swap, table, place, (b * batch, (b + 1) * batch))
        for off in range(1, chips):
            part_copy(off, b).start()
    part_got[chip] = part_send[chip]
    meta_got[chip] = meta_send[...]
    sums[...] = jnp.zeros_like(sums)
    norms[...] = jnp.zeros_like(norms)
    for off in range(1, chips):
        cls_copy(off).wait_recv()
        cross_copy(off).start()
        pass_copy(off, 0).start()
    for off in range(1, chips):
        meta_copy(off).wait()

    def lanes_of(src, b):
        return pl.ds(pl.multiple_of((src * BATCHES + b) * slots, slots), slots)

    @pl.loop(0, chips)
    def _(src):
        meta = meta_got[src].astype(F32).T[:particles].astype(jnp.int32)
        ctf_got[src] = ctf_rows(meta, priors, ctf_ref[...])
        for b in range(BATCHES):
            found = class_hits(meta[b * batch : (b + 1) * batch], priors, classes)
            hits[src, b] = found.astype(BF16)
            hits_t[:, lanes_of(src, b)] = found.T.astype(BF16)

    for off in range(1, chips):
        cross_got(off).wait_recv()
        pass_copy(off, 1).start()
    for off in range(1, chips):
        cls_copy(off).wait_send()
        cross_copy(off).wait_send()
    for off in range(chips):
        for h in range(2):
            pass_copy(off, h).wait_send()
            pass_got(off, h).wait_recv()

    def score(src, b):
        ctf = ctf_got[src, frames_of(b)]
        real, imag = 0.0, 0.0
        for s in range(share):
            part = part_got[src, s, frames_of(b)].astype(F32)
            part = part * column(ctf, first_cycle[s] + chip_step * chip)
            scaled[src, s, frames_of(b)] = part.astype(BF16)
            table = cls_got[:, s].reshape(classes, width)
            picked = jnp.dot(hits[src, b], table, preferred_element_type=F32)
            picked = picked.reshape(priors, batch, width)
            pc, ps = part[None, :, :harm], part[None, :, harm:]
            cc, cs = picked[:, :, :harm], picked[:, :, harm:]
            real = real + (pc * cc + ps * cs)
            imag = imag + (pc * cs - ps * cc)
        score_send[src, b, :, :, :harm] = real.astype(BF16)
        score_send[src, b, :, :, harm:] = imag.astype(BF16)

    for b in range(BATCHES):
        score(chip, b)
    for b in range(BATCHES):

        @pl.loop(1, chips)
        def _(off):
            part_copy(off, b).wait_recv()
            score(chip_at(off), b)
            score_copy(off, b).start()

    for b in range(BATCHES):
        joined = score_send[chip, b].astype(F32)
        for off in range(1, chips):
            score_copy(off, b).wait_recv()
            joined = joined + score_got[chip_at(off), b].astype(F32)
        scores = table_product(joined.reshape(slots, width), inverse_ref[...])
        scores = scores.reshape(priors, batch, angles)
        highest = jnp.max(jnp.max(scores, axis=0), axis=1, keepdims=True)
        total = jnp.sum(jnp.exp(scores - highest[None]), axis=0)
        log_total = highest + jnp.log(jnp.sum(total, axis=1, keepdims=True))
        weights = jnp.exp(scores - log_total[None]).reshape(slots, angles)
        spectrum = table_product(weights, forward_ref[...])
        spec_send[b] = spectrum.astype(BF16).reshape(priors, batch, width)
        for off in range(1, chips):
            spec_copy(off, b).start()
        spec_got[chip, b] = spec_send[b]

    half = doms * run
    other_half, own_half = ((1 - core) * half, core * half) if deliver else (0, 0)

    def slot_terms(src, b, s):
        spectrum = spec_got[src, b]
        wc, ws = spectrum[:, :, :harm], spectrum[:, :, harm:]
        part = scaled[src, s, frames_of(b)][None]
        pc, ps = part[:, :, :harm], part[:, :, harm:]
        both = jnp.concatenate([pc * wc + ps * ws, ps * wc - pc * ws], axis=2)
        return both.reshape(slots, width)

    def add(src, b):
        chosen = hits_t[:, lanes_of(src, b)]
        ctf = ctf_got[src, frames_of(b)]
        square = (ctf * ctf)[None] * spec_got[src, b, :, :, :1].astype(F32)
        parts = jnp.concatenate(split(square.reshape(slots, cycles)), axis=1)
        norms[...] += jnp.dot(chosen, parts, preferred_element_type=F32)
        for i in range(sums.shape[0]):
            sums[i] += jnp.dot(
                chosen, slot_terms(src, b, other_half + i), preferred_element_type=F32
            )

    for b in range(BATCHES):
        add(chip, b)
    for b in range(BATCHES):

        @pl.loop(1, chips)
        def _(off):
            spec_copy(off, b).wait_recv()
            add(chip_at(off), b)

    for b in range(BATCHES):
        for off in range(1, chips):
            part_copy(off, b).wait_send()
            score_copy(off, b).wait_send()
            spec_copy(off, b).wait_send()
    norms[:, :cycles] += norms[:, cycles:]

    if not deliver:
        sum_out[...] = sums[...].astype(BF16)
        norm_out[...] = norms[:, :cycles]
        return

    mine = pl.multiple_of(me * owned, owned)
    other = pl.multiple_of(sibling[1] * owned, owned)
    order = sorted(range(doms), key=lambda a: (a == 0, abs(a - doms // 2)))

    def half_copy(a):
        at = pl.ds(peer(a, 0)[0] * run, run)
        return remote(half_send.at[at], half_got.at[at], half_sem, (a,), sibling)

    for a in order:
        at = pl.ds(peer(a, 0)[0] * run, run)
        half_send[at] = sums[at].astype(BF16)
        half_copy(a).start()
    half_norm[...] = norms[pl.ds(other, owned), :]
    norm_half = remote(half_norm, half_norm_got, half_sem, (doms,), sibling)
    norm_half.start()

    def sum_copy(a, b):
        to = peer(a, b)
        start = pl.multiple_of(to[1] * owned, owned)
        src = sum_send.at[pl.ds(to[0] * run, run), pl.ds(start, owned), :]
        return remote(src, sum_got.at[dom, me], sum_sem, (a, b), to)

    def norm_copy(a):
        return remote(norm_send, norm_got.at[dom], norm_sem, (a,), peer(a, 0))

    for a in order:
        first = peer(a, 0)[0] * run
        own = []
        for one in range(run):
            for src in range(chips):
                for b in range(BATCHES):
                    at = pl.ds((src * BATCHES + b) * slots, slots)
                    terms[one, at, :] = slot_terms(src, b, own_half + first + one)
            own.append(jnp.dot(hits_t[...], terms[one], preferred_element_type=F32))
        half_copy(a).wait()
        for one in range(run):
            both = own[one] + half_got[first + one].astype(F32)
            sum_send[first + one] = both.astype(BF16)
        for b in range(owners):
            if (a, b) in offsets:
                sum_copy(a, b).start()
        if a == order[0]:
            norm_half.wait()
            norm_send[...] = norms[pl.ds(mine, owned), :] + half_norm_got[...]
            for to in range(1, doms):
                norm_copy(to).start()
    sum_got[dom, me] = sum_send[pl.ds(dom * run, run), pl.ds(mine, owned), :]
    norm_got[dom] = norm_send[...]
    for a, b in offsets:
        sum_copy(a, b).wait()
    for a in range(1, doms):
        norm_copy(a).wait()


def finish_body(cycles, sum_ref, norm_ref, out_ref, low, high):
    doms, owners, run, owned, width = sum_ref.shape
    harm = width // 2
    held = owners * run
    dom = lax.axis_index("dom")
    norms = norm_ref[0, :, :cycles]
    for a in range(1, doms):
        norms = norms + norm_ref[a, :, :cycles]
    for c in range(owners):
        for one in range(run):
            cycle = c * run + one
            result = sum_ref[0, c, one].astype(F32)
            for a in range(1, doms):
                result = result + sum_ref[a, c, one].astype(F32)
            result = result / (column(norms, dom * held + cycle) + 1.0)
            at = pl.ds(cycle, owned, stride=held)
            low[at, :] = result[:, :harm]
            high[at, :] = result[:, harm:]
    out_ref[:, :harm] = low[...]
    out_ref[:, harm:] = high[...]


def on_device(doms, images, references, ctf_table, defocus, priors):
    owners = lax.axis_size("cls")
    particles, cycles, angles = images.shape
    owned = references.shape[0]
    classes = owners * owned
    prior_count = priors.shape[1]
    chips = owners // CORES
    share = cycles // chips
    width = angles // 2 * 2
    held = cycles // doms
    deliver = held % owners == 0
    run = max(held // owners, 1)
    forward, inverse = (jnp.asarray(t) for t in angle_tables(angles))
    swap = jnp.asarray(swap_matrix(), BF16)
    if deliver:
        shapes = [
            jax.ShapeDtypeStruct((doms, owners, run, owned, width), BF16),
            jax.ShapeDtypeStruct((doms, owned, 2 * cycles), F32),
        ]
    else:
        shapes = [
            jax.ShapeDtypeStruct((share, classes, width), BF16),
            jax.ShapeDtypeStruct((classes, cycles), F32),
        ]
    batch = particles // BATCHES
    slots = (BATCHES, prior_count, batch, width)
    rows = prior_count * batch
    sums = (share, classes, width)
    half = (doms * run, classes, width)
    pair_sem = pltpu.SemaphoreType.DMA((2, chips))
    batch_sem = pltpu.SemaphoreType.DMA((2, chips, BATCHES))
    done = pl.pallas_call(
        functools.partial(body, doms, chips, prior_count, deliver),
        out_shape=shapes,
        in_specs=[pl.BlockSpec(memory_space=pl.ANY)] + [VMEM] * 7,
        out_specs=[VMEM] * len(shapes),
        scratch_shapes=[
            pltpu.VMEM(images.shape, BF16),
            pltpu.VMEM((chips, share, particles, width), BF16),
            pltpu.VMEM((chips, share, particles, width), BF16),
            pltpu.VMEM((chips, share, owned, width), BF16),
            pltpu.VMEM((owners, share, owned, width), BF16),
            pltpu.VMEM((16, 128), jnp.int32),
            pltpu.VMEM((chips, 16, 128), jnp.int32),
            pltpu.VMEM((chips, share, particles, width), BF16),
            pltpu.VMEM((chips, particles, cycles), F32),
            pltpu.VMEM((chips, BATCHES, rows, classes), BF16),
            pltpu.VMEM((classes, chips * BATCHES * rows), BF16),
            pltpu.VMEM((run, chips * BATCHES * rows, width), BF16),
            pltpu.VMEM((chips,) + slots, BF16),
            pltpu.VMEM((chips,) + slots, BF16),
            pltpu.VMEM(slots, BF16),
            pltpu.VMEM((chips,) + slots, BF16),
            pltpu.VMEM(half if deliver else sums, F32),
            pltpu.VMEM((classes, 2 * cycles), F32),
            pltpu.VMEM(half, BF16),
            pltpu.VMEM(half, BF16),
            pltpu.VMEM((owned, 2 * cycles), F32),
            pltpu.VMEM((owned, 2 * cycles), F32),
            pltpu.VMEM(half, BF16),
            pltpu.VMEM((owned, 2 * cycles), F32),
            pltpu.SemaphoreType.DMA,
            pair_sem,
            pair_sem,
            pltpu.SemaphoreType.DMA((2, chips, 2)),
            pair_sem,
            batch_sem,
            batch_sem,
            batch_sem,
            pltpu.SemaphoreType.DMA((2, doms + 1)),
            pltpu.SemaphoreType.DMA((2, doms, owners)),
            pltpu.SemaphoreType.DMA((2, doms)),
        ],
        compiler_params=pltpu.CompilerParams(
            collective_id=1, has_side_effects=True, vmem_limit_bytes=LIMIT
        ),
    )(images, references, priors.T, defocus[None, :], ctf_table, swap, forward, inverse)
    if deliver:
        done = pl.pallas_call(
            functools.partial(finish_body, cycles),
            out_shape=jax.ShapeDtypeStruct((owned * held, width), F32),
            in_specs=[VMEM] * 2,
            out_specs=VMEM,
            scratch_shapes=[pltpu.VMEM((owned * held, width // 2), F32)] * 2,
            compiler_params=pltpu.CompilerParams(vmem_limit_bytes=LIMIT),
        )(*done)
        return done.reshape(owned, held, width)
    sums, norms = done
    me = lax.axis_index("cls")
    chip = me // CORES
    mine = chip * share + jnp.arange(share)
    placed = jnp.zeros((cycles, classes, width), F32).at[mine].set(sums.astype(F32))
    placed = lax.psum_scatter(placed, "dom", scatter_dimension=0, tiled=True)
    placed = lax.psum_scatter(placed, "cls", scatter_dimension=1, tiled=True)
    rows = jnp.arange(classes)[:, None] // (CORES * owned)
    norms = jnp.where(rows == chip, norms, 0.0)
    norms = lax.psum_scatter(norms, "dom", scatter_dimension=1, tiled=True)
    norms = lax.psum_scatter(norms, "cls", scatter_dimension=0, tiled=True)
    return placed.transpose(1, 0, 2) / (norms + 1.0)[:, :, None]


def solution(mesh):
    return jax.shard_map(
        functools.partial(on_device, mesh.shape["dom"]),
        mesh=mesh,
        in_specs=(
            P(("dom", "cls"), None, None),
            P("cls", None, None),
            P(),
            P(("dom", "cls")),
            P(("dom", "cls"), None),
        ),
        out_specs=P("cls", "dom", None),
        check_vma=False,
    )
```

```python
import functools

import jax
import jax.numpy as jnp
import numpy as np
from jax import lax
from jax.experimental import pallas as pl
from jax.experimental.pallas import tpu as pltpu
from jax.sharding import PartitionSpec as P

MESH = pl.DeviceIdType.MESH
VMEM = pl.BlockSpec(memory_space=pltpu.VMEM)
LIMIT = 56 * 1024 * 1024
F32 = jnp.float32
BF16 = jnp.bfloat16
EXACT = lax.Precision.HIGHEST
TILE = 16
CORES = 2
BATCHES = 2


def angle_tables(angles):
    harm_count = angles // 2
    phase = np.arange(angles)[:, None] * np.arange(harm_count)[None, :] % angles
    grid = 2.0 * np.pi / angles * phase
    cosine, sine = np.cos(grid), np.sin(grid)
    forward = np.concatenate([cosine, sine], axis=1)
    weight = np.where(np.arange(harm_count) == 0, 1.0, 2.0)[:, None] / angles
    inverse = np.concatenate([cosine.T * weight, -sine.T * weight], axis=0)
    return forward.astype(np.float32), inverse.astype(np.float32)


def swap_matrix():
    rows = np.arange(TILE * TILE)
    swap = np.zeros((TILE * TILE, TILE * TILE), np.float32)
    swap[rows, rows % TILE * TILE + rows // TILE] = 1.0
    return swap


def harmonics(src, dst, swap, table, place, frames):
    cycles, angles = src.shape[1:]
    for first in range(0, cycles, TILE):
        for frame in range(*frames, TILE):
            block = src[frame : frame + TILE, first : first + TILE, :]
            block = block.reshape(TILE * TILE, angles)
            block = jnp.dot(swap, block, preferred_element_type=F32).astype(BF16)
            out = jnp.dot(block, table, preferred_element_type=F32).astype(BF16)
            for r in range(TILE):
                chip, s = place(first + r)
                dst[chip, s, frame : frame + TILE, :] = out[r * TILE : (r + 1) * TILE]


def column(rows, index):
    lanes = lax.broadcasted_iota(jnp.int32, rows.shape, 1)
    return jnp.sum(jnp.where(lanes == index, rows, 0.0), axis=1, keepdims=True)


def class_hits(meta, priors, classes):
    lanes = lax.broadcasted_iota(jnp.int32, (meta.shape[0], classes), 1)
    return jnp.concatenate(
        [(meta[:, j : j + 1] == lanes).astype(F32) for j in range(priors)], axis=0
    )


def split(rows):
    high = rows.astype(BF16)
    return high, (rows - high.astype(F32)).astype(BF16)


def table_product(rows, table):
    high, low = split(rows)
    table_high, table_low = split(table)
    total = jnp.dot(high, table_low, preferred_element_type=F32)
    total = total + jnp.dot(low, table_high, preferred_element_type=F32)
    return total + jnp.dot(high, table_high, preferred_element_type=F32)


def ctf_rows(meta, priors, table):
    groups = table.shape[0]
    lanes = lax.broadcasted_iota(jnp.int32, (meta.shape[0], groups), 1)
    hits = (meta[:, priors : priors + 1] == lanes).astype(F32)
    return jnp.dot(hits, table, precision=EXACT, preferred_element_type=F32)


def body(
    doms,
    chips,
    priors,
    deliver,
    img_ref,
    ref_ref,
    priors_ref,
    defocus_ref,
    ctf_ref,
    swap_ref,
    forward_ref,
    inverse_ref,
    *rest,
):
    if deliver:
        sum_got, norm_got, rest = rest[0], rest[1], rest[2:]
    else:
        sum_out, norm_out, rest = rest[0], rest[1], rest[2:]
    (
        img_got,
        part_send,
        part_got,
        cls_send,
        cls_got,
        meta_send,
        meta_got,
        scaled,
        ctf_got,
        ctf_wide,
        hits,
        hits_t,
        terms,
        score_send,
        score_got,
        spec_send,
        spec_got,
        sums,
        norms,
        half_send,
        half_got,
        half_norm,
        half_norm_got,
        sum_send,
        norm_send,
        img_sem,
        cls_sem,
        cross_sem,
        pass_sem,
        meta_sem,
        part_sem,
        score_sem,
        spec_sem,
        half_sem,
        sum_sem,
        norm_sem,
    ) = rest
    dom, me = lax.axis_index("dom"), lax.axis_index("cls")
    chip, core = me // CORES, me % CORES
    sibling = (dom, me + 1 - 2 * core)
    particles, cycles, angles = img_ref.shape
    batch = particles // BATCHES
    slots = priors * batch
    owned = ref_ref.shape[0]
    owners = chips * CORES
    classes = owners * owned
    share = cycles // chips
    harm = angles // 2
    width = 2 * harm
    held = cycles // doms
    run = max(held // owners, 1)

    def place(r):
        if not deliver:
            return r // share, r % share
        to, chip, half, one = r // held, r % held // (CORES * run), r // run % CORES, r % run
        return chip, (half * doms + to) * run + one

    places = {place(r): r for r in range(cycles)}
    first_cycle = [places[0, s] for s in range(share)]
    chip_step = places[1, 0] - places[0, 0]

    barrier = pltpu.get_barrier_semaphore()
    offsets = [(a, b) for a in range(doms) for b in range(owners)][1:]

    def peer(a, b):
        return (lax.rem(dom + a, doms), lax.rem(me + b, owners))

    def chip_at(off):
        number, bit = 0, 1
        while bit < chips:
            ours, flip = chip // bit % 2, off // bit % 2
            number = number + bit * (ours + flip - 2 * ours * flip)
            bit *= 2
        return number

    def remote(src, dst, sem, at, device):
        return pltpu.make_async_remote_copy(
            src_ref=src,
            dst_ref=dst,
            send_sem=sem.at[(0,) + at],
            recv_sem=sem.at[(1,) + at],
            device_id=device,
            device_id_type=MESH,
        )

    def same_core(off):
        return (dom, chip_at(off) * CORES + core)

    upper = dom % 2
    partner = (dom + 1 - 2 * upper, me)
    part_share = share // 2

    def cycle_half(h):
        return pl.ds((upper + h - 2 * upper * h) * part_share, part_share)

    def cls_copy(off):
        src = cls_send.at[chip_at(off), cycle_half(0)]
        return remote(src, cls_got.at[me, cycle_half(0)], cls_sem, (off,), same_core(off))

    def cross_copy(off):
        slot = cls_got.at[chip_at(off) * CORES + core, cycle_half(0)]
        return remote(slot, slot, cross_sem, (off,), partner)

    def cross_got(off):
        slot = cls_got.at[chip_at(off) * CORES + core, cycle_half(1)]
        return remote(slot, slot, cross_sem, (off,), partner)

    def pass_copy(off, h):
        slot = cls_got.at[chip_at(off) * CORES + core, cycle_half(h)]
        return remote(slot, slot, pass_sem, (off, h), sibling)

    def pass_got(off, h):
        slot = cls_got.at[chip_at(off) * CORES + 1 - core, cycle_half(h)]
        return remote(slot, slot, pass_sem, (off, h), sibling)

    def meta_copy(off):
        return remote(meta_send, meta_got.at[chip], meta_sem, (off,), same_core(off))

    def frames_of(b):
        return pl.ds(b * batch, batch)

    def part_copy(off, b):
        return remote(
            part_send.at[chip_at(off), :, frames_of(b), :],
            part_got.at[chip, :, frames_of(b), :],
            part_sem,
            (off, b),
            same_core(off),
        )

    def score_copy(off, b):
        return remote(
            score_send.at[chip_at(off), b],
            score_got.at[chip, b],
            score_sem,
            (off, b),
            same_core(off),
        )

    def spec_copy(off, b):
        return remote(spec_send.at[b], spec_got.at[chip, b], spec_sem, (off, b), same_core(off))

    images = pltpu.make_async_copy(img_ref, img_got, img_sem)
    images.start()
    for a, b in offsets:
        pl.semaphore_signal(barrier, inc=1, device_id=peer(a, b), device_id_type=MESH)
    meta_send[...] = jnp.zeros_like(meta_send)
    meta_send[:priors, :particles] = priors_ref[...]
    meta_send[priors : priors + 1, :particles] = defocus_ref[...]
    table = forward_ref[...].astype(BF16)
    swap = swap_ref[...]
    harmonics(ref_ref, cls_send, swap, table, place, (0, owned))
    cls_got[me] = cls_send[chip]
    pl.semaphore_wait(barrier, len(offsets))
    for off in range(1, chips):
        meta_copy(off).start()
        cls_copy(off).start()
    for h in range(2):
        pass_copy(0, h).start()
    images.wait()
    for b in range(BATCHES):
        harmonics(img_got, part_send, swap, table, place, (b * batch, (b + 1) * batch))
        for off in range(1, chips):
            part_copy(off, b).start()
    part_got[chip] = part_send[chip]
    meta_got[chip] = meta_send[...]
    sums[...] = jnp.zeros_like(sums)
    norms[...] = jnp.zeros_like(norms)
    for off in range(1, chips):
        cls_copy(off).wait_recv()
        cross_copy(off).start()
        pass_copy(off, 0).start()
    for off in range(1, chips):
        meta_copy(off).wait()

    def lanes_of(src, b):
        return pl.ds(pl.multiple_of((src * BATCHES + b) * slots, slots), slots)

    @pl.loop(0, chips)
    def _(src):
        meta = meta_got[src].astype(F32).T[:particles].astype(jnp.int32)
        ctf = ctf_rows(meta, priors, ctf_ref[...])
        ctf_got[src] = ctf
        for s in range(share):
            one = column(ctf, first_cycle[s] + chip_step * chip)
            ctf_wide[src, s] = jnp.broadcast_to(one, (particles, harm))
        for b in range(BATCHES):
            found = class_hits(meta[b * batch : (b + 1) * batch], priors, classes)
            hits[src, b] = found.astype(BF16)
            hits_t[:, lanes_of(src, b)] = found.T.astype(BF16)

    for off in range(1, chips):
        cross_got(off).wait_recv()
        pass_copy(off, 1).start()
    for off in range(1, chips):
        cls_copy(off).wait_send()
        cross_copy(off).wait_send()
    for off in range(chips):
        for h in range(2):
            pass_copy(off, h).wait_send()
            pass_got(off, h).wait_recv()

    def score(src, b):
        real, imag = 0.0, 0.0
        for s in range(share):
            wide = ctf_wide[src, s, frames_of(b)]
            part = part_got[src, s, frames_of(b)].astype(F32)
            part = part * jnp.concatenate([wide, wide], axis=1)
            scaled[src, s, frames_of(b)] = part.astype(BF16)
            table = cls_got[:, s].reshape(classes, width)
            picked = jnp.dot(hits[src, b], table, preferred_element_type=F32)
            picked = picked.reshape(priors, batch, width)
            pc, ps = part[None, :, :harm], part[None, :, harm:]
            cc, cs = picked[:, :, :harm], picked[:, :, harm:]
            real = real + (pc * cc + ps * cs)
            imag = imag + (pc * cs - ps * cc)
        score_send[src, b, :, :, :harm] = real.astype(BF16)
        score_send[src, b, :, :, harm:] = imag.astype(BF16)

    for b in range(BATCHES):
        score(chip, b)
    for b in range(BATCHES):

        @pl.loop(1, chips)
        def _(off):
            part_copy(off, b).wait_recv()
            score(chip_at(off), b)
            score_copy(off, b).start()

    for b in range(BATCHES):
        joined = score_send[chip, b].astype(F32)
        for off in range(1, chips):
            score_copy(off, b).wait_recv()
            joined = joined + score_got[chip_at(off), b].astype(F32)
        scores = table_product(joined.reshape(slots, width), inverse_ref[...])
        scores = scores.reshape(priors, batch, angles)
        highest = jnp.max(jnp.max(scores, axis=0), axis=1, keepdims=True)
        total = jnp.sum(jnp.exp(scores - highest[None]), axis=0)
        log_total = highest + jnp.log(jnp.sum(total, axis=1, keepdims=True))
        weights = jnp.exp(scores - log_total[None]).reshape(slots, angles)
        spectrum = table_product(weights, forward_ref[...])
        spec_send[b] = spectrum.astype(BF16).reshape(priors, batch, width)
        for off in range(1, chips):
            spec_copy(off, b).start()
        spec_got[chip, b] = spec_send[b]

    half = doms * run
    other_half, own_half = ((1 - core) * half, core * half) if deliver else (0, 0)

    def slot_terms(src, b, s):
        spectrum = spec_got[src, b]
        wc, ws = spectrum[:, :, :harm], spectrum[:, :, harm:]
        part = scaled[src, s, frames_of(b)][None]
        pc, ps = part[:, :, :harm], part[:, :, harm:]
        both = jnp.concatenate([pc * wc + ps * ws, ps * wc - pc * ws], axis=2)
        return both.reshape(slots, width)

    def add(src, b):
        chosen = hits_t[:, lanes_of(src, b)]
        ctf = ctf_got[src, frames_of(b)]
        square = (ctf * ctf)[None] * spec_got[src, b, :, :, :1].astype(F32)
        parts = jnp.concatenate(split(square.reshape(slots, cycles)), axis=1)
        norms[...] += jnp.dot(chosen, parts, preferred_element_type=F32)
        for i in range(sums.shape[0]):
            sums[i] += jnp.dot(
                chosen, slot_terms(src, b, other_half + i), preferred_element_type=F32
            )

    for b in range(BATCHES):
        add(chip, b)
    for b in range(BATCHES):

        @pl.loop(1, chips)
        def _(off):
            spec_copy(off, b).wait_recv()
            add(chip_at(off), b)

    for b in range(BATCHES):
        for off in range(1, chips):
            part_copy(off, b).wait_send()
            score_copy(off, b).wait_send()
            spec_copy(off, b).wait_send()
    norms[:, :cycles] += norms[:, cycles:]

    if not deliver:
        sum_out[...] = sums[...].astype(BF16)
        norm_out[...] = norms[:, :cycles]
        return

    mine = pl.multiple_of(me * owned, owned)
    other = pl.multiple_of(sibling[1] * owned, owned)
    order = sorted(range(doms), key=lambda a: (a == 0, abs(a - doms // 2)))

    def half_copy(a):
        at = pl.ds(peer(a, 0)[0] * run, run)
        return remote(half_send.at[at], half_got.at[at], half_sem, (a,), sibling)

    for a in order:
        at = pl.ds(peer(a, 0)[0] * run, run)
        half_send[at] = sums[at].astype(BF16)
        half_copy(a).start()
    half_norm[...] = norms[pl.ds(other, owned), :]
    norm_half = remote(half_norm, half_norm_got, half_sem, (doms,), sibling)
    norm_half.start()

    def sum_copy(a, b):
        to = peer(a, b)
        start = pl.multiple_of(to[1] * owned, owned)
        src = sum_send.at[pl.ds(to[0] * run, run), pl.ds(start, owned), :]
        return remote(src, sum_got.at[dom, me], sum_sem, (a, b), to)

    def norm_copy(a):
        return remote(norm_send, norm_got.at[dom], norm_sem, (a,), peer(a, 0))

    for a in order:
        first = peer(a, 0)[0] * run
        own = []
        for one in range(run):
            for src in range(chips):
                for b in range(BATCHES):
                    at = pl.ds((src * BATCHES + b) * slots, slots)
                    terms[one, at, :] = slot_terms(src, b, own_half + first + one)
            own.append(jnp.dot(hits_t[...], terms[one], preferred_element_type=F32))
        half_copy(a).wait()
        for one in range(run):
            both = own[one] + half_got[first + one].astype(F32)
            sum_send[first + one] = both.astype(BF16)
        for b in range(owners):
            if (a, b) in offsets:
                sum_copy(a, b).start()
        if a == order[0]:
            norm_half.wait()
            norm_send[...] = norms[pl.ds(mine, owned), :] + half_norm_got[...]
            for to in range(1, doms):
                norm_copy(to).start()
    sum_got[dom, me] = sum_send[pl.ds(dom * run, run), pl.ds(mine, owned), :]
    norm_got[dom] = norm_send[...]
    for a, b in offsets:
        sum_copy(a, b).wait()
    for a in range(1, doms):
        norm_copy(a).wait()


def finish_body(cycles, sum_ref, norm_ref, out_ref, low, high):
    doms, owners, run, owned, width = sum_ref.shape
    harm = width // 2
    held = owners * run
    dom = lax.axis_index("dom")
    norms = norm_ref[0, :, :cycles]
    for a in range(1, doms):
        norms = norms + norm_ref[a, :, :cycles]
    for c in range(owners):
        for one in range(run):
            cycle = c * run + one
            result = sum_ref[0, c, one].astype(F32)
            for a in range(1, doms):
                result = result + sum_ref[a, c, one].astype(F32)
            result = result / (column(norms, dom * held + cycle) + 1.0)
            at = pl.ds(cycle, owned, stride=held)
            low[at, :] = result[:, :harm]
            high[at, :] = result[:, harm:]
    out_ref[:, :harm] = low[...]
    out_ref[:, harm:] = high[...]


def on_device(doms, images, references, ctf_table, defocus, priors):
    owners = lax.axis_size("cls")
    particles, cycles, angles = images.shape
    owned = references.shape[0]
    classes = owners * owned
    prior_count = priors.shape[1]
    chips = owners // CORES
    share = cycles // chips
    width = angles // 2 * 2
    held = cycles // doms
    deliver = held % owners == 0
    run = max(held // owners, 1)
    forward, inverse = (jnp.asarray(t) for t in angle_tables(angles))
    swap = jnp.asarray(swap_matrix(), BF16)
    if deliver:
        shapes = [
            jax.ShapeDtypeStruct((doms, owners, run, owned, width), BF16),
            jax.ShapeDtypeStruct((doms, owned, 2 * cycles), F32),
        ]
    else:
        shapes = [
            jax.ShapeDtypeStruct((share, classes, width), BF16),
            jax.ShapeDtypeStruct((classes, cycles), F32),
        ]
    batch = particles // BATCHES
    slots = (BATCHES, prior_count, batch, width)
    rows = prior_count * batch
    sums = (share, classes, width)
    half = (doms * run, classes, width)
    pair_sem = pltpu.SemaphoreType.DMA((2, chips))
    batch_sem = pltpu.SemaphoreType.DMA((2, chips, BATCHES))
    done = pl.pallas_call(
        functools.partial(body, doms, chips, prior_count, deliver),
        out_shape=shapes,
        in_specs=[pl.BlockSpec(memory_space=pl.ANY)] + [VMEM] * 7,
        out_specs=[VMEM] * len(shapes),
        scratch_shapes=[
            pltpu.VMEM(images.shape, BF16),
            pltpu.VMEM((chips, share, particles, width), BF16),
            pltpu.VMEM((chips, share, particles, width), BF16),
            pltpu.VMEM((chips, share, owned, width), BF16),
            pltpu.VMEM((owners, share, owned, width), BF16),
            pltpu.VMEM((16, 128), jnp.int32),
            pltpu.VMEM((chips, 16, 128), jnp.int32),
            pltpu.VMEM((chips, share, particles, width), BF16),
            pltpu.VMEM((chips, particles, cycles), F32),
            pltpu.VMEM((chips, share, particles, width // 2), F32),
            pltpu.VMEM((chips, BATCHES, rows, classes), BF16),
            pltpu.VMEM((classes, chips * BATCHES * rows), BF16),
            pltpu.VMEM((run, chips * BATCHES * rows, width), BF16),
            pltpu.VMEM((chips,) + slots, BF16),
            pltpu.VMEM((chips,) + slots, BF16),
            pltpu.VMEM(slots, BF16),
            pltpu.VMEM((chips,) + slots, BF16),
            pltpu.VMEM(half if deliver else sums, F32),
            pltpu.VMEM((classes, 2 * cycles), F32),
            pltpu.VMEM(half, BF16),
            pltpu.VMEM(half, BF16),
            pltpu.VMEM((owned, 2 * cycles), F32),
            pltpu.VMEM((owned, 2 * cycles), F32),
            pltpu.VMEM(half, BF16),
            pltpu.VMEM((owned, 2 * cycles), F32),
            pltpu.SemaphoreType.DMA,
            pair_sem,
            pair_sem,
            pltpu.SemaphoreType.DMA((2, chips, 2)),
            pair_sem,
            batch_sem,
            batch_sem,
            batch_sem,
            pltpu.SemaphoreType.DMA((2, doms + 1)),
            pltpu.SemaphoreType.DMA((2, doms, owners)),
            pltpu.SemaphoreType.DMA((2, doms)),
        ],
        compiler_params=pltpu.CompilerParams(
            collective_id=1, has_side_effects=True, vmem_limit_bytes=LIMIT
        ),
    )(images, references, priors.T, defocus[None, :], ctf_table, swap, forward, inverse)
    if deliver:
        done = pl.pallas_call(
            functools.partial(finish_body, cycles),
            out_shape=jax.ShapeDtypeStruct((owned * held, width), F32),
            in_specs=[VMEM] * 2,
            out_specs=VMEM,
            scratch_shapes=[pltpu.VMEM((owned * held, width // 2), F32)] * 2,
            compiler_params=pltpu.CompilerParams(vmem_limit_bytes=LIMIT),
        )(*done)
        return done.reshape(owned, held, width)
    sums, norms = done
    me = lax.axis_index("cls")
    chip = me // CORES
    mine = chip * share + jnp.arange(share)
    placed = jnp.zeros((cycles, classes, width), F32).at[mine].set(sums.astype(F32))
    placed = lax.psum_scatter(placed, "dom", scatter_dimension=0, tiled=True)
    placed = lax.psum_scatter(placed, "cls", scatter_dimension=1, tiled=True)
    rows = jnp.arange(classes)[:, None] // (CORES * owned)
    norms = jnp.where(rows == chip, norms, 0.0)
    norms = lax.psum_scatter(norms, "dom", scatter_dimension=1, tiled=True)
    norms = lax.psum_scatter(norms, "cls", scatter_dimension=0, tiled=True)
    return placed.transpose(1, 0, 2) / (norms + 1.0)[:, :, None]


def solution(mesh):
    return jax.shard_map(
        functools.partial(on_device, mesh.shape["dom"]),
        mesh=mesh,
        in_specs=(
            P(("dom", "cls"), None, None),
            P("cls", None, None),
            P(),
            P(("dom", "cls")),
            P(("dom", "cls"), None),
        ),
        out_specs=P("cls", "dom", None),
        check_vma=False,
    )
```
